256 devices in a mesh: seq: 32 (over x, y, core), head: 8 (over z).
Axes of the slice: x: 4, y: 4, z: 8, core: 2. Of those that a mesh axis runs over, the one named last changes fastest.
Arguments:
- queries: bfloat16 [16384, 4096], P('seq', 'head'), may hold values from -6 to 6
- keys: bfloat16 [16384, 4096], P('seq', 'head'), may hold values from -6 to 6
- values: bfloat16 [16384, 4096], P('seq', 'head'), may hold values from -6 to 6
- w_out: bfloat16 [4096, 4096], P(None, 'head'), may hold values from -0.125 to 0.125
- grad_out: bfloat16 [16384, 4096], P('seq', 'head'), may hold values from -6 to 6
Outputs:
- layer_out: bfloat16 [16384, 4096], P('seq', 'head')
- grad_queries: bfloat16 [16384, 4096], P('seq', 'head')
- grad_keys: bfloat16 [16384, 4096], P('seq', 'head')
- grad_values: bfloat16 [16384, 4096], P('seq', 'head')
- grad_w_out: float32 [4096, 4096], P('seq', 'head')
The draws below stay inside these ranges and needn't reach their ends.
All inputs are finite; a program needn't handle non-finite values.
Results may differ from the reference program's by a relative error of at most 0.0051.
Values may be sent and summed in bfloat16 or wider, within the bound.
No kernel may reach another device: no remote copies, remote signals or barrier semaphores. Data moves between devices by JAX's collectives and lax.ppermute only.
A program may use at most 128 MiB of HBM per device.

```python
import jax
import jax.numpy as jnp
from jax import lax

D = 4096
H = 32
DH = 128
TOK_DEV = 512
HD = 4096
TOKENS = 16384
N_SEQ = 32


def raised(drawn, rng, source, target, parts, factor):
    owner, partner = [(jnp.arange(drawn.shape[position]) // (drawn.shape[position] // parts)).reshape([-1 if axis == position else 1 for axis in range(drawn.ndim)]) for position in (source, target)]
    chosen = jax.random.permutation(rng, parts)[partner]
    strong = (owner == chosen) | (owner == (partner + parts // 2) % parts)
    return jnp.where(strong, factor * drawn, drawn)


def steps_of(rng, shape, split, low, largest):
    level, own = 1.0, jax.random.fold_in(rng, 6)
    for dim, blocks in split:
        heights = jnp.exp(jax.random.uniform(jax.random.fold_in(own, dim), (blocks,), jnp.float32, low / len(split), largest / len(split)))
        level = level * jnp.repeat(heights, shape[dim] // blocks).reshape([-1 if axis == dim else 1 for axis in range(len(shape))])
    return level


def bell_draw(key, extent, deviation, limit, pieces=(), held_as=jnp.bfloat16):
    drawn = deviation * jax.random.normal(key, extent, jnp.float32)
    if pieces:
        drawn = drawn * steps_of(key, extent, pieces, -0.22, 0.18)
    return jnp.clip(drawn, -limit, limit).astype(held_as)


def gaussian_with(stream_key, shape, deviation, reach, split, heavy, dtype=jnp.bfloat16):
    result = deviation * jax.random.normal(stream_key, shape, jnp.float32)
    if split:
        result = result * steps_of(stream_key, shape, split, -0.22, 0.18)
    return jnp.clip(raised(result, jax.random.fold_in(stream_key, 3), *heavy), -reach, reach).astype(dtype)


def setup_inputs(seed: int = 0) -> dict:
    arg_keys = jax.random.split(jax.random.key(seed), 6)
    queries = bell_draw(arg_keys[0], (TOKENS, HD), 1.0, 6.0, ((0, 32), (1, 8)))
    keys = bell_draw(arg_keys[1], (TOKENS, HD), 1.0, 6.0, ((0, 32), (1, 8)))
    values = bell_draw(arg_keys[2], (TOKENS, HD), 1.0, 6.0, ((0, 32), (1, 8)))
    w_out = gaussian_with(arg_keys[3], (D, HD), HD ** -0.5, 0.125, ((1, 8),), (1, 0, 8, 2.0))
    grad_out = gaussian_with(arg_keys[4], (TOKENS, D), 1.0, 6.0, ((0, 32), (1, 8)), (0, 1, 32, 2.75))
    return dict(queries=queries, keys=keys, values=values, w_out=w_out, grad_out=grad_out)


epsilon = 1e-06

def split_heads(array):
    return array.astype(jnp.float32).reshape(N_SEQ, TOK_DEV, H, DH)

def product(form, left, right):
    return jnp.einsum(form, left, right, precision=lax.Precision.HIGHEST)

def reference(queries, keys, values, w_out, grad_out):
    query_all = split_heads(queries)
    key_all = split_heads(keys)
    value_all = split_heads(values)
    causal = jnp.tril(jnp.ones((TOK_DEV, TOK_DEV), jnp.float32))

    def forward_step(state, block):
        query_blk, key_blk, value_blk = block
        scores = product('thd,shd->hts', query_blk, key_blk) * causal
        output = product('hts,she->the', scores, value_blk) + product('thd,hde->the', query_blk, state)
        return (state + product('shd,she->hde', key_blk, value_blk), (output, state))
    zero_state = jnp.zeros((H, DH, DH), jnp.float32)
    _, (mixed, prefixes) = lax.scan(forward_step, zero_state, (query_all, key_all, value_all))
    inverse = lax.rsqrt(lax.optimization_barrier(jnp.mean(mixed * mixed, axis=-1, keepdims=True)) + epsilon)
    normed = mixed * inverse
    attn = normed.reshape(TOKENS, HD).astype(jnp.bfloat16)
    layer_out = lax.dot_general(attn, w_out, (((1,), (1,)), ((), ())), preferred_element_type=jnp.float32).astype(jnp.bfloat16)
    d_attn = jnp.dot(grad_out, w_out, preferred_element_type=jnp.float32).reshape(N_SEQ, TOK_DEV, H, DH)
    d_mixed = inverse * (d_attn - normed * lax.optimization_barrier(jnp.mean(d_attn * normed, axis=-1, keepdims=True)))
    grad_mixed = d_mixed.astype(jnp.bfloat16).astype(jnp.float32)

    def backward_step(later_grads, block):
        query_blk, key_blk, value_blk, grad_blk, prefix_blk = block
        scores = product('thd,shd->hts', query_blk, key_blk) * causal
        grad_scores = product('the,she->hts', grad_blk, value_blk) * causal
        grad_query = product('hts,shd->thd', grad_scores, key_blk) + product('the,hde->thd', grad_blk, prefix_blk)
        grad_key = product('hts,thd->shd', grad_scores, query_blk) + product('she,hde->shd', value_blk, later_grads)
        grad_value = product('hts,the->she', scores, grad_blk) + product('shd,hde->she', key_blk, later_grads)
        updated = later_grads + product('thd,the->hde', query_blk, grad_blk)
        return (updated, (grad_query, grad_key, grad_value))
    _, (grad_query_all, grad_key_all, grad_value_all) = lax.scan(backward_step, zero_state, (query_all, key_all, value_all, grad_mixed, prefixes), reverse=True)
    grad_queries = grad_query_all.reshape(TOKENS, HD).astype(jnp.bfloat16)
    grad_keys = grad_key_all.reshape(TOKENS, HD).astype(jnp.bfloat16)
    grad_values = grad_value_all.reshape(TOKENS, HD).astype(jnp.bfloat16)
    grad_w_out = lax.dot_general(grad_out, attn, (((0,), (0,)), ((), ())), preferred_element_type=jnp.float32)
    return (layer_out, grad_queries, grad_keys, grad_values, grad_w_out)
```

```python
import functools

import jax
import jax.numpy as jnp
from jax import lax
from jax.experimental import pallas as pl
from jax.experimental.pallas import tpu as pltpu
from jax.sharding import PartitionSpec as P

DH = 128
epsilon = 1e-06
MIB = 1 << 20
bf16, f32 = jnp.bfloat16, jnp.float32


def dot(a, b, left, right):
    return lax.dot_general(a, b, (((left,), (right,)), ((), ())), preferred_element_type=f32)


def split(x):
    high = x.astype(bf16)
    return high, (x - high.astype(f32)).astype(bf16)


def dot2(parts, b, left, right):
    return dot(parts[0], b, left, right) + dot(parts[1], b, left, right)


def dot2r(a, parts, left, right):
    return dot(a, parts[0], left, right) + dot(a, parts[1], left, right)


def shape(dims, dtype):
    return jax.ShapeDtypeStruct(dims, dtype)


def call(body, outs, args, name, flops, scalars=0, vmem=40):
    in_specs = [pl.BlockSpec(memory_space=pltpu.SMEM)] * scalars
    in_specs += [pl.BlockSpec(memory_space=pltpu.VMEM)] * (len(args) - scalars)
    size = sum(a.size * a.dtype.itemsize for a in list(args) + list(outs))
    return pl.pallas_call(
        body,
        out_shape=tuple(outs),
        in_specs=in_specs,
        out_specs=tuple([pl.BlockSpec(memory_space=pltpu.VMEM)] * len(outs)),
        compiler_params=pltpu.CompilerParams(vmem_limit_bytes=vmem * MIB),
        cost_estimate=pl.CostEstimate(flops=flops, bytes_accessed=size, transcendentals=0),
        name=name,
    )(*args)


def head(i):
    return slice(i * DH, (i + 1) * DH)


def state_body(left, right, out):
    for h in range(out.shape[0]):
        out[h] = dot(left[:, head(h)], right[:, head(h)], 0, 0)


def prefix_body(reverse, parts, out):
    count = parts.shape[0]
    state = jnp.zeros(parts.shape[1:], f32)
    for step in range(count):
        i = count - 1 - step if reverse else step
        out[i] = state
        state = state + parts[i]


def lower_mask(rows):
    return lax.broadcasted_iota(jnp.int32, (rows, rows), 0) >= lax.broadcasted_iota(
        jnp.int32, (rows, rows), 1
    )


def forward_body(q, k, v, prefix, attn, attn_t, mixed_out):
    rows = q.shape[0]
    mask = lower_mask(rows)
    for h in range(prefix.shape[0]):
        qh, kh, vh = q[:, head(h)], k[:, head(h)], v[:, head(h)]
        scores = split(jnp.where(mask, dot(qh, kh, 1, 1), 0.0))
        mixed = dot2(scores, vh, 1, 0) + dot2r(qh, split(prefix[h]), 1, 0)
        inverse = lax.rsqrt(jnp.mean(mixed * mixed, axis=-1, keepdims=True) + epsilon)
        normed = mixed * inverse
        mixed_out[:, head(h)] = mixed
        attn[:, head(h)] = normed.astype(bf16)
        attn_t[head(h), :] = normed.T.astype(bf16)


def project_body(offsets, me, w, mixed, q, *rest):
    blocks, (d_mixed, grads) = rest[:-2], rest[-2:]
    ring = w.shape[0] // w.shape[1]
    wide = w.shape[1]
    half = q.shape[0] // 2
    top = bottom = None
    for block, (offset, part) in zip(blocks, offsets):
        source = lax.rem(me[0] + offset, ring)
        weight = w[pl.ds(pl.multiple_of(source * wide, wide), wide), :]
        if part != 1:
            term = dot(block[0:half, :], weight, 1, 0)
            top = term if top is None else top + term
        if part != 0:
            rows = block[half:, :] if part == 2 else block[...]
            term = dot(rows, weight, 1, 0)
            bottom = term if bottom is None else bottom + term
    for h in range(grads.shape[0]):
        total = None
        for place, d_part in ((slice(0, half), top), (slice(half, 2 * half), bottom)):
            d_attn = d_part[:, head(h)]
            m = mixed[place, head(h)]
            inverse = lax.rsqrt(jnp.mean(m * m, axis=-1, keepdims=True) + epsilon)
            normed = m * inverse
            d_m = inverse * (d_attn - normed * jnp.mean(d_attn * normed, axis=-1, keepdims=True))
            d_m = d_m.astype(bf16)
            d_mixed[place, head(h)] = d_m
            term = dot(q[place, head(h)], d_m, 0, 0)
            total = term if total is None else total + term
        grads[h] = total


def backward_body(q, k, v, d_mixed, prefix, later, grad_q, grad_k, grad_v):
    rows = q.shape[0]
    low = lower_mask(rows)
    high = lax.broadcasted_iota(jnp.int32, (rows, rows), 0) <= lax.broadcasted_iota(
        jnp.int32, (rows, rows), 1
    )
    for h in range(prefix.shape[0]):
        qh, kh, vh, dh = q[:, head(h)], k[:, head(h)], v[:, head(h)], d_mixed[:, head(h)]
        before, after = split(prefix[h]), split(later[h])
        d_scores = split(jnp.where(low, dot(dh, vh, 1, 1), 0.0))
        grad_q[:, head(h)] = (dot2(d_scores, kh, 1, 0) + dot2r(dh, before, 1, 1)).astype(bf16)
        d_scores_t = split(jnp.where(high, dot(vh, dh, 1, 1), 0.0))
        grad_k[:, head(h)] = (dot2(d_scores_t, qh, 1, 0) + dot2r(vh, after, 1, 1)).astype(bf16)
        scores_t = split(jnp.where(high, dot(kh, qh, 1, 1), 0.0))
        grad_v[:, head(h)] = (dot2(scores_t, dh, 1, 0) + dot2r(kh, after, 1, 0)).astype(bf16)


def weight_body(offsets, ring, me, attn_t, *rest):
    blocks, (keep, send) = rest[:-2], rest[-2:]
    half = attn_t.shape[1] // 2
    wide = 128
    first = me[1] == 0
    for blocks_of, offset in offsets:
        source = lax.rem(me[0] + offset, ring)
        if len(blocks_of) == 1:
            terms = dot(attn_t[...], blocks[blocks_of[0]][...], 1, 0)
        else:
            terms = dot(attn_t[:, 0:half], blocks[blocks_of[0]][...], 1, 0) + dot(
                attn_t[:, half:], blocks[blocks_of[1]][...], 1, 0
            )
        for j in range(terms.shape[1] // (2 * wide)):
            even = terms[:, 2 * j * wide : (2 * j + 1) * wide]
            odd = terms[:, (2 * j + 1) * wide : (2 * j + 2) * wide]
            place = source * (terms.shape[1] // (2 * wide)) + j
            keep[place] = jnp.where(first, even, odd)
            send[place] = jnp.where(first, odd, even).astype(bf16)


def sum_body(parts, out):
    total = parts[0].astype(f32)
    for i in range(1, parts.shape[0]):
        total = total + parts[i].astype(f32)
    out[...] = total.T


def first_body(me, attn, w, top, bottom):
    half = attn.shape[0] // 2
    terms = dot(attn[...], w[...], 1, 1).astype(bf16)
    top[...] = terms[0:half]
    bottom[...] = terms[half:]


def step_body(me, attn, w, from_left, from_right, to_right, to_left):
    half = attn.shape[0] // 2
    terms = dot(attn[...], w[...], 1, 1)

    def put(source, target, top):
        if source.shape[0] == target.shape[0]:
            target[...] = (terms + source[...].astype(f32)).astype(bf16)
        else:
            place, other = slice(0, half), slice(half, 2 * half)
            if not top:
                place, other = other, place
            target[place, :] = (terms[place] + source[...].astype(f32)).astype(bf16)
            target[other, :] = terms[other].astype(bf16)

    @pl.when(pl.program_id(0) == 0)
    def _():
        put(from_left, to_right, True)

    @pl.when(pl.program_id(0) == 1)
    def _():
        put(from_right, to_left, False)


def last_body(me, attn, w, from_left, from_right, out):
    terms = dot(attn[...], w[...], 1, 1)
    out[...] = (terms + from_left[...].astype(f32) + from_right[...].astype(f32)).astype(bf16)


def ring_call(body, outs, me, attn, w, rest, offsets, name):
    ring = w.shape[0] // attn.shape[0]
    wide = w.shape[0] // ring

    def whole(a):
        return pl.BlockSpec(a.shape, lambda i, me: (0,) * len(a.shape))

    def weight(i, me):
        offset = offsets[0] if len(offsets) == 1 else jnp.where(i == 0, offsets[0], offsets[1])
        return (lax.rem(me[0] + offset, ring), 0)

    size = attn.size * (len(rest) + len(outs) + len(offsets) + 1) * 2
    return pl.pallas_call(
        body,
        grid_spec=pltpu.PrefetchScalarGridSpec(
            num_scalar_prefetch=1,
            grid=(len(offsets),),
            in_specs=[whole(attn), pl.BlockSpec((wide, w.shape[1]), weight)]
            + [whole(a) for a in rest],
            out_specs=tuple(whole(o) for o in outs),
        ),
        out_shape=tuple(outs),
        compiler_params=pltpu.CompilerParams(vmem_limit_bytes=24 * MIB),
        cost_estimate=pl.CostEstimate(
            flops=2 * attn.size * wide * len(offsets), bytes_accessed=size, transcendentals=0
        ),
        name=name,
    )(me, attn, w, *rest)


def shift(x, axis, amount):
    count = lax.axis_size(axis)
    return lax.ppermute(x, axis, [(i, (i + amount) % count) for i in range(count)])


def across(state, reverse, name):
    count = lax.axis_size("seq")
    dims = state.shape
    parts = state.reshape(count, -1, dims[-1])
    parts = lax.all_to_all(parts, "seq", 0, 0, tiled=True)
    (sums,) = call(
        functools.partial(prefix_body, reverse), [shape(parts.shape, f32)], [parts], name, parts.size
    )
    sums = lax.all_to_all(sums, "seq", 0, 0, tiled=True)
    return sums.reshape(dims)


def per_device(queries, keys, values, w_out, grad_out):
    length, features = queries.shape
    heads = features // DH
    half = length // 2
    ring = lax.axis_size("head")
    count = lax.axis_size("seq")
    me = jnp.stack([lax.axis_index("head"), lax.rem(lax.axis_index("seq"), 2)]).astype(jnp.int32)
    block = shape((length, features), bf16)
    half_block = shape((half, features), bf16)
    states = shape((heads, DH, DH), f32)
    pair_flops = 2 * length * features * DH

    right = left = grad_out
    blocks, offsets = [grad_out], [(0, 2)]
    for hop in range(1, ring // 2):
        right, left = shift(right, "head", 1), shift(left, "head", -1)
        blocks += [right, left]
        offsets += [(ring - hop, 2), (hop, 2)]
    top, bottom = shift(right[:half], "head", 1), shift(left[half:], "head", -1)
    blocks += [top, bottom]
    offsets += [(ring // 2, 0), (ring // 2, 1)]

    (local_state,) = call(state_body, [states], [keys, values], "state", pair_flops)
    prefix = across(local_state, False, "prefix")
    attn, attn_t, mixed = call(
        forward_body,
        [block, shape((features, length), bf16), shape((length, features), f32)],
        [queries, keys, values, prefix],
        "forward",
        12 * pair_flops,
    )

    to_right, to_left = ring_call(
        first_body, [half_block, half_block], me, attn, w_out, [], [ring // 2], "out_first"
    )
    for hop in range(ring // 2 - 1, 0, -1):
        from_left, from_right = shift(to_right, "head", 1), shift(to_left, "head", -1)
        to_right, to_left = ring_call(
            step_body,
            [block, block],
            me,
            attn,
            w_out,
            [from_left, from_right],
            [hop, ring - hop],
            "out_step",
        )
    from_left, from_right = shift(to_right, "head", 1), shift(to_left, "head", -1)
    (layer_out,) = ring_call(
        last_body, [block], me, attn, w_out, [from_left, from_right], [0], "out_last"
    )

    d_mixed, local_grads = call(
        functools.partial(project_body, offsets),
        [block, states],
        [me, w_out, mixed, queries] + blocks,
        "project",
        2 * length * features * features * ring,
        scalars=1,
    )
    later = across(local_grads, True, "suffix")
    grad_q, grad_k, grad_v = call(
        backward_body,
        [block, block, block],
        [queries, keys, values, d_mixed, prefix, later],
        "backward",
        36 * pair_flops,
    )

    grouped = [([i], offsets[i][0]) for i in range(ring - 1)] + [([ring - 1, ring], ring // 2)]
    pieces = (count // 2, features, w_out.shape[0] // count)
    keep, send = call(
        functools.partial(weight_body, grouped, ring),
        [shape(pieces, f32), shape(pieces, bf16)],
        [me, attn_t] + blocks,
        "weight",
        2 * length * features * features * ring,
        scalars=1,
    )
    received = lax.ppermute(send, "seq", [(i, i ^ 1) for i in range(count)])
    both = (keep + received.astype(f32)).astype(bf16)
    groups = [[2 * chip + core for chip in range(count // 2)] for core in range(2)]
    terms = lax.all_to_all(both, "seq", 0, 0, axis_index_groups=groups, tiled=True)
    (grad_w_out,) = call(
        sum_body, [shape((pieces[2], pieces[1]), f32)], [terms], "weight_sum", terms.size
    )
    return layer_out, grad_q, grad_k, grad_v, grad_w_out


def solution(mesh):
    return jax.shard_map(
        per_device,
        mesh=mesh,
        in_specs=(
            P("seq", "head"),
            P("seq", "head"),
            P("seq", "head"),
            P(None, "head"),
            P("seq", "head"),
        ),
        out_specs=(
            P("seq", "head"),
            P("seq", "head"),
            P("seq", "head"),
            P("seq", "head"),
            P("seq", "head"),
        ),
        check_vma=False,
    )
```

```python
import functools

import jax
import jax.numpy as jnp
from jax import lax
from jax.experimental import pallas as pl
from jax.experimental.pallas import tpu as pltpu
from jax.sharding import PartitionSpec as P

DH = 128
epsilon = 1e-06
VMEM = 63 << 20
bf16, f32 = jnp.bfloat16, jnp.float32


def dot(a, b, left, right):
    return lax.dot_general(a, b, (((left,), (right,)), ((), ())), preferred_element_type=f32)


def split(x):
    high = x.astype(bf16)
    return high, (x - high.astype(f32)).astype(bf16)


def dot2(parts, b, left, right):
    return dot(parts[0], b, left, right) + dot(parts[1], b, left, right)


def dot2r(a, parts, left, right):
    return dot(a, parts[0], left, right) + dot(a, parts[1], left, right)


def shape(dims, dtype):
    return jax.ShapeDtypeStruct(dims, dtype)


def call(body, outs, args, name, weight=1, scalars=0):
    in_specs = [pl.BlockSpec(memory_space=pltpu.SMEM)] * scalars
    in_specs += [pl.BlockSpec(memory_space=pltpu.VMEM)] * (len(args) - scalars)
    return pl.pallas_call(
        body,
        out_shape=tuple(outs),
        in_specs=in_specs,
        out_specs=tuple([pl.BlockSpec(memory_space=pltpu.VMEM)] * len(outs)),
        compiler_params=pltpu.CompilerParams(vmem_limit_bytes=VMEM),
        cost_estimate=pl.CostEstimate(flops=weight * 10**10, bytes_accessed=1000, transcendentals=0),
        name=name,
    )(*args)


def head(i):
    return slice(i * DH, (i + 1) * DH)


def state_body(left, right, out):
    for h in range(out.shape[0]):
        out[h] = dot(left[:, head(h)], right[:, head(h)], 0, 0)


def prefix_body(reverse, parts, out):
    count = parts.shape[0]
    state = jnp.zeros(parts.shape[1:], f32)
    for step in range(count):
        i = count - 1 - step if reverse else step
        out[i] = state
        state = state + parts[i]


def lower_mask(rows):
    return lax.broadcasted_iota(jnp.int32, (rows, rows), 0) >= lax.broadcasted_iota(
        jnp.int32, (rows, rows), 1
    )


def forward_body(q, k, v, prefix, attn, attn_t, mixed_out):
    rows = q.shape[0]
    mask = lower_mask(rows)
    for h in range(prefix.shape[0]):
        qh, kh, vh = q[:, head(h)], k[:, head(h)], v[:, head(h)]
        scores = split(jnp.where(mask, dot(qh, kh, 1, 1), 0.0))
        mixed = dot2(scores, vh, 1, 0) + dot2r(qh, split(prefix[h]), 1, 0)
        inverse = lax.rsqrt(jnp.mean(mixed * mixed, axis=-1, keepdims=True) + epsilon)
        normed = mixed * inverse
        mixed_out[:, head(h)] = mixed
        attn[:, head(h)] = normed.astype(bf16)
        attn_t[head(h), :] = normed.T.astype(bf16)


def block_term(block, place, weight):
    rows = block[...] if block.shape[0] == place.stop - place.start else block[place, :]
    return dot(rows, weight, 1, 0)


def add_blocks(offsets, me, w, blocks, place, start):
    wide = w.shape[1]
    ring = w.shape[0] // wide
    total = start
    for block, (offset, part) in zip(blocks, offsets):
        if part is not None and part != place:
            continue
        source = lax.rem(me[0] + offset, ring)
        weight = w[pl.ds(pl.multiple_of(source * wide, wide), wide), :]
        term = block_term(block, place, weight)
        total = term if total is None else total + term
    return total


def project_early_body(offsets, me, w, *rest):
    blocks, out = rest[:-1], rest[-1]
    place = slice(0, out.shape[0])
    out[...] = add_blocks(offsets, me, w, blocks, place, None)


def project_body(offsets, me, w, early, mixed, q, *rest):
    blocks, (d_mixed, grads) = rest[:-2], rest[-2:]
    half = q.shape[0] // 2
    totals = [None] * grads.shape[0]
    for place in (slice(0, half), slice(half, 2 * half)):
        d_part = add_blocks(offsets, me, w, blocks, place, early[place, :])
        for h in range(grads.shape[0]):
            d_attn = d_part[:, head(h)]
            m = mixed[place, head(h)]
            inverse = lax.rsqrt(jnp.mean(m * m, axis=-1, keepdims=True) + epsilon)
            normed = m * inverse
            d_m = inverse * (d_attn - normed * jnp.mean(d_attn * normed, axis=-1, keepdims=True))
            d_m = d_m.astype(bf16)
            d_mixed[place, head(h)] = d_m
            term = dot(q[place, head(h)], d_m, 0, 0)
            totals[h] = term if totals[h] is None else totals[h] + term
    for h in range(grads.shape[0]):
        grads[h] = totals[h]


def backward_body(q, k, v, d_mixed, prefix, grad_q, part_k, part_v):
    rows = q.shape[0]
    low = lower_mask(rows)
    high = lax.broadcasted_iota(jnp.int32, (rows, rows), 0) <= lax.broadcasted_iota(
        jnp.int32, (rows, rows), 1
    )
    for h in range(prefix.shape[0]):
        qh, kh, vh, dh = q[:, head(h)], k[:, head(h)], v[:, head(h)], d_mixed[:, head(h)]
        d_scores = split(jnp.where(low, dot(dh, vh, 1, 1), 0.0))
        grad_q[:, head(h)] = (
            dot2(d_scores, kh, 1, 0) + dot2r(dh, split(prefix[h]), 1, 1)
        ).astype(bf16)
        d_scores_t = split(jnp.where(high, dot(vh, dh, 1, 1), 0.0))
        part_k[:, head(h)] = dot2(d_scores_t, qh, 1, 0)
        scores_t = split(jnp.where(high, dot(kh, qh, 1, 1), 0.0))
        part_v[:, head(h)] = dot2(scores_t, dh, 1, 0)


def finish_body(k, v, part_k, part_v, later, grad_k, grad_v):
    for h in range(later.shape[0]):
        after = split(later[h])
        grad_k[:, head(h)] = (part_k[:, head(h)] + dot2r(v[:, head(h)], after, 1, 1)).astype(bf16)
        grad_v[:, head(h)] = (part_v[:, head(h)] + dot2r(k[:, head(h)], after, 1, 0)).astype(bf16)


def weight_body(me, attn_t, *rest):
    blocks, (keep, send) = rest[:-2], rest[-2:]
    wide = keep.shape[2]
    half = attn_t.shape[1] // 2
    first = me[1] == 0
    groups = blocks[0].shape[1] // (2 * wide)
    place = 0
    while blocks:
        if blocks[0].shape[0] == 2 * half:
            terms, blocks = dot(attn_t[...], blocks[0][...], 1, 0), blocks[1:]
        else:
            terms = dot(attn_t[:, 0:half], blocks[0][...], 1, 0)
            terms = terms + dot(attn_t[:, half:], blocks[1][...], 1, 0)
            blocks = blocks[2:]
        for j in range(groups):
            even = terms[:, 2 * j * wide : (2 * j + 1) * wide]
            odd = terms[:, (2 * j + 1) * wide : (2 * j + 2) * wide]
            keep[place] = jnp.where(first, even, odd)
            send[place] = jnp.where(first, odd, even).astype(bf16)
            place += 1


def pair_body(offsets, ring, me, *rest):
    sources, out = rest[:-1], rest[-1]
    groups = out.shape[0] // ring
    at = 0
    for keep, received in zip(sources[0::2], sources[1::2]):
        for i in range(keep.shape[0] // groups):
            source = lax.rem(me[0] + offsets[at], ring)
            for j in range(groups):
                term = keep[groups * i + j] + received[groups * i + j].astype(f32)
                out[source * groups + j] = term.astype(bf16)
            at += 1


def sum_body(parts, out):
    total = parts[0].astype(f32)
    for i in range(1, parts.shape[0]):
        total = total + parts[i].astype(f32)
    out[...] = total.T


def out_body(attn, w, out):
    out[...] = dot(attn[...], w[...], 1, 1).astype(bf16)


def out_call(attn, w):
    rows, features = attn.shape
    return pl.pallas_call(
        out_body,
        grid=(w.shape[0] // features,),
        in_specs=[
            pl.BlockSpec((rows, features), lambda i: (0, 0)),
            pl.BlockSpec((features, features), lambda i: (i, 0)),
        ],
        out_specs=pl.BlockSpec((rows, features), lambda i: (i, 0)),
        out_shape=shape((rows * w.shape[0] // features, features), bf16),
        compiler_params=pltpu.CompilerParams(vmem_limit_bytes=VMEM),
        cost_estimate=pl.CostEstimate(flops=1000, bytes_accessed=1000, transcendentals=0),
        name="out_terms",
    )(attn, w)


def shift(x, axis, amount):
    count = lax.axis_size(axis)
    return lax.ppermute(x, axis, [(i, (i + amount) % count) for i in range(count)])


def per_device(queries, keys, values, w_out, grad_out):
    length, features = queries.shape
    heads = features // DH
    half = length // 2
    ring = lax.axis_size("head")
    count = lax.axis_size("seq")
    me = jnp.stack([lax.axis_index("head"), lax.rem(lax.axis_index("seq"), 2)]).astype(jnp.int32)
    block = shape((length, features), bf16)
    wide_block = shape((length, features), f32)
    states = shape((heads, DH, DH), f32)
    tie = lax.optimization_barrier

    def exchange(parts):
        return lax.all_to_all(parts, "seq", 0, 0, tiled=True)

    def sums(parts, reverse, name):
        body = functools.partial(prefix_body, reverse)
        return call(body, [shape(parts.shape, f32)], [parts], name)[0]

    def pieces_of(state):
        return state.reshape(count, -1, DH)

    def swap(x):
        return lax.ppermute(x, "seq", [(i, i ^ 1) for i in range(count)])

    def weight(blocks, number, name):
        dims = (number * count // (2 * ring), features, w_out.shape[0] // count)
        outs = [shape(dims, f32), shape(dims, bf16)]
        keep, send = call(weight_body, outs, [me, attn_t] + blocks, name, scalars=1)
        return [keep, swap(send)]

    right, left = shift(grad_out, "head", 1), shift(grad_out, "head", -1)
    (local_state,) = call(state_body, [states], [keys, values], "state")
    parts = exchange(pieces_of(local_state))
    right, left, parts = tie((right, left, parts))
    blocks, offsets = [grad_out, right, left], [(0, None), (ring - 1, None), (1, None)]
    right, left = shift(right, "head", 1), shift(left, "head", -1)
    prefix = exchange(sums(parts, False, "prefix"))
    right, left, prefix = tie((right, left, prefix))
    prefix = prefix.reshape(states.shape)
    blocks += [right, left]
    offsets += [(ring - 2, None), (2, None)]
    right, left = shift(right, "head", 1), shift(left, "head", -1)
    attn, attn_t, mixed = call(
        forward_body,
        [block, shape((features, length), bf16), wide_block],
        [queries, keys, values, prefix],
        "forward",
    )
    terms = out_call(attn, w_out)
    layer_out = lax.psum_scatter(terms, "head", scatter_dimension=0, tiled=True)
    me, terms = tie((me, terms))
    early = call(
        functools.partial(project_early_body, offsets),
        [wide_block],
        [me, w_out] + blocks,
        "project_early",
        scalars=1,
    )[0]
    early, attn_t = tie((early, attn_t))
    pairs = weight(blocks, len(blocks), "weight_early")
    right, left, early, pairs[0] = tie((right, left, early, pairs[0]))
    top, bottom = shift(right[:half], "head", 1), shift(left[half:], "head", -1)
    last_blocks = [right, left, top, bottom]
    last_offsets = [
        (ring - 3, None),
        (3, None),
        (ring // 2, slice(0, half)),
        (ring // 2, slice(half, length)),
    ]
    pairs += weight(last_blocks, 3, "weight_late")
    early, pairs[2] = tie((early, pairs[2]))
    d_mixed, local_grads = call(
        functools.partial(project_body, last_offsets),
        [block, states],
        [me, w_out, early, mixed, queries] + last_blocks,
        "project",
        scalars=1,
    )
    parts = exchange(pieces_of(local_grads))
    order = [offset for offset, _ in (offsets + last_offsets)[:ring]]
    dims = (count // 2, features, w_out.shape[0] // count)
    both = call(
        functools.partial(pair_body, order, ring),
        [shape(dims, bf16)],
        [me] + pairs,
        "pair_add",
        scalars=1,
    )[0]
    parts, both = tie((parts, both))
    groups = [[2 * chip + core for chip in range(count // 2)] for core in range(2)]
    both = lax.all_to_all(both, "seq", 0, 0, axis_index_groups=groups, tiled=True)
    grad_q, part_k, part_v = call(
        backward_body,
        [block, wide_block, wide_block],
        [queries, keys, values, d_mixed, prefix],
        "backward",
    )
    parts, grad_q, part_k, part_v = tie((parts, grad_q, part_k, part_v))
    later = exchange(sums(parts, True, "suffix")).reshape(states.shape)
    grad_k, grad_v = call(
        finish_body, [block, block], [keys, values, part_k, part_v, later], "finish"
    )
    grad_w_out = call(sum_body, [shape((dims[2], dims[1]), f32)], [both], "weight_sum")[0]
    return layer_out, grad_q, grad_k, grad_v, grad_w_out


def solution(mesh):
    return jax.shard_map(
        per_device,
        mesh=mesh,
        in_specs=(
            P("seq", "head"),
            P("seq", "head"),
            P("seq", "head"),
            P(None, "head"),
            P("seq", "head"),
        ),
        out_specs=(
            P("seq", "head"),
            P("seq", "head"),
            P("seq", "head"),
            P("seq", "head"),
            P("seq", "head"),
        ),
        check_vma=False,
    )
```

```python
import functools

import jax
import jax.numpy as jnp
from jax import lax
from jax.experimental import pallas as pl
from jax.experimental.pallas import tpu as pltpu
from jax.sharding import PartitionSpec as P

DH = 128
epsilon = 1e-06
VMEM = 62 << 20
WORK = 10**9
LIGHT = 0
bf16, f32 = jnp.bfloat16, jnp.float32


def dot(a, b, left, right):
    return lax.dot_general(a, b, (((left,), (right,)), ((), ())), preferred_element_type=f32)


def split(x):
    high = x.astype(bf16)
    return high, (x - high.astype(f32)).astype(bf16)


def dot2(parts, b, left, right):
    return dot(parts[0], b, left, right) + dot(parts[1], b, left, right)


def dot2r(a, parts, left, right):
    return dot(a, parts[0], left, right) + dot(a, parts[1], left, right)


def shape(dims, dtype):
    return jax.ShapeDtypeStruct(dims, dtype)


def cost(weight=1):
    return pl.CostEstimate(flops=int(weight * WORK), bytes_accessed=1000, transcendentals=0)


def whole(dims):
    return pl.BlockSpec(tuple(dims), lambda *_: (0,) * len(dims))


def call(body, outs, args, name, grid=None, specs=None, scalars=0, scratch=(), weight=1):
    specs = specs or ([None] * (len(args) - scalars), [None] * len(outs))
    ins = [s or whole(a.shape) for s, a in zip(specs[0], args[scalars:])]
    outs_specs = tuple(s or whole(o.shape) for s, o in zip(specs[1], outs))
    return pl.pallas_call(
        body,
        grid_spec=pltpu.PrefetchScalarGridSpec(
            num_scalar_prefetch=scalars,
            grid=grid or (1,),
            in_specs=ins,
            out_specs=outs_specs,
            scratch_shapes=scratch,
        ),
        out_shape=tuple(outs),
        compiler_params=pltpu.CompilerParams(vmem_limit_bytes=VMEM),
        cost_estimate=cost(weight),
        name=name,
    )(*args)


def head(i):
    return slice(i * DH, (i + 1) * DH)


def columns(rows):
    return pl.BlockSpec((rows, DH), lambda h: (0, h))


def per_head():
    return pl.BlockSpec((1, DH, DH), lambda h: (h, 0, 0))


def state_body(left, right, out):
    out[0] = dot(left[...], right[...], 0, 0)


def prefix_body(reverse, parts, out):
    count = parts.shape[0]
    state = jnp.zeros(parts.shape[1:], f32)
    for step in range(count):
        i = count - 1 - step if reverse else step
        out[i] = state
        state = state + parts[i]


def place(rows):
    return (
        lax.broadcasted_iota(jnp.int32, (rows, rows), 0),
        lax.broadcasted_iota(jnp.int32, (rows, rows), 1),
    )


def forward_body(q, k, v, prefix, attn, attn_t, mixed_out):
    row, column = place(q.shape[0])
    scores = split(jnp.where(row >= column, dot(q[...], k[...], 1, 1), 0.0))
    mixed = dot2(scores, v[...], 1, 0) + dot2r(q[...], split(prefix[0]), 1, 0)
    inverse = lax.rsqrt(jnp.mean(mixed * mixed, axis=-1, keepdims=True) + epsilon)
    normed = mixed * inverse
    mixed_out[...] = mixed
    attn[...] = normed.astype(bf16)
    attn_t[...] = normed.T.astype(bf16)


def project_body(blocks, w, mixed, q, d_mixed, grads, total):
    step = pl.program_id(0)
    wide = w.shape[1]
    term = None
    for i in range(blocks.shape[0]):
        part = dot(blocks[i], w[i * wide : (i + 1) * wide, :], 1, 0)
        term = part if term is None else term + part

    @pl.when(step == 0)
    def _():
        total[...] = term

    @pl.when(step > 0)
    def _():
        total[...] += term

    @pl.when(step == pl.num_programs(0) - 1)
    def _():
        for h in range(grads.shape[0]):
            d_attn, m = total[:, head(h)], mixed[:, head(h)]
            inverse = lax.rsqrt(jnp.mean(m * m, axis=-1, keepdims=True) + epsilon)
            normed = m * inverse
            d_m = inverse * (d_attn - normed * jnp.mean(d_attn * normed, axis=-1, keepdims=True))
            d_m = d_m.astype(bf16)
            d_mixed[:, head(h)] = d_m
            grads[h] = dot(q[:, head(h)], d_m, 0, 0)


def backward_body(q, k, v, d_mixed, prefix, grad_q, part_k, part_v):
    row, column = place(q.shape[0])
    q, k, v, d = q[...], k[...], v[...], d_mixed[...]
    d_scores = split(jnp.where(row >= column, dot(d, v, 1, 1), 0.0))
    grad_q[...] = (dot2(d_scores, k, 1, 0) + dot2r(d, split(prefix[0]), 1, 1)).astype(bf16)
    d_scores_t = split(jnp.where(row <= column, dot(v, d, 1, 1), 0.0))
    part_k[...] = dot2(d_scores_t, q, 1, 0)
    scores_t = split(jnp.where(row <= column, dot(k, q, 1, 1), 0.0))
    part_v[...] = dot2(scores_t, d, 1, 0)


def finish_body(k, v, part_k, part_v, later, grad_k, grad_v):
    after = split(later[0])
    grad_k[...] = (part_k[...] + dot2r(v[...], after, 1, 1)).astype(bf16)
    grad_v[...] = (part_v[...] + dot2r(k[...], after, 1, 0)).astype(bf16)


def weight_body(me, attn_t, block, keep, send):
    wide = keep.shape[2]
    first = me[1] == 0
    terms = dot(attn_t[...], block[0], 1, 0)
    for j in range(keep.shape[0]):
        even = terms[:, 2 * j * wide : (2 * j + 1) * wide]
        odd = terms[:, (2 * j + 1) * wide : (2 * j + 2) * wide]
        keep[j] = jnp.where(first, even, odd)
        send[j] = jnp.where(first, odd, even).astype(bf16)


ORDER = (2, 1, 3, 0)


def pair_body(me, keep, received, *outs):
    far, near = outs[:4], outs[4:]
    side = keep.shape[1]
    half = keep.shape[2] // 2
    for step, dx in enumerate(ORDER):

        @pl.when(pl.program_id(0) == step)
        def _(dx=dx):
            for dy in range(side):
                source = lax.rem(me[3] + dy, side)
                term = (keep[0, source] + received[0, source].astype(f32)).astype(bf16)
                for kind, first, second, rows in (
                    (0, dx, dy, term[:half]),
                    (1, dy, dx, term[half:]),
                ):
                    if first == 2:
                        far[2 * kind + second // 2][second % 2] = rows
                    else:
                        near[3 * kind + (1, 3, 0).index(first)][second] = rows


def turn_body(*refs):
    count = len(refs) // 3
    near, got, outs = refs[:count], refs[count : 2 * count], refs[2 * count :]
    for i in range(count):
        half = got[i].shape[0]
        into, other = (slice(0, half), slice(half, 2 * half))[:: 1 if i % 2 == 0 else -1]
        term = near[i][into].astype(f32) + got[i][...].astype(f32)
        outs[i][into] = term.astype(outs[i].dtype)
        outs[i][other] = near[i][other]


def cross_body(own_a, own_b, *refs):
    got, outs = refs[:4], refs[4:]
    for kind, own in enumerate((own_a, own_b)):
        left, right = got[2 * kind], got[2 * kind + 1]
        far, near = outs[2 * kind : 2 * kind + 2], outs[4 + 3 * kind : 7 + 3 * kind]
        half = far[0].shape[0]
        for i in range(own.shape[0]):
            term = own[i].astype(f32) + left[i].astype(f32) + right[i].astype(f32)
            if i == 2:
                far[0][...] = term[:half]
                far[1][...] = term[half:]
            else:
                near[(1, 3, 0).index(i)][...] = term


def close_body(own_a, own_b, *refs):
    got, out = refs[:4], refs[4]
    half = own_a.shape[0]
    for kind, own in enumerate((own_a, own_b)):
        term = own[...] + got[2 * kind][...] + got[2 * kind + 1][...]
        out[:, kind * half : (kind + 1) * half] = term.T


def first_body(me, attn, w, top, bottom):
    half = attn.shape[0] // 2
    terms = dot(attn[...], w[...], 1, 1).astype(bf16)
    top[...] = terms[0:half]
    bottom[...] = terms[half:]


def step_body(me, attn, w, from_left, from_right, to_right, to_left):
    half = attn.shape[0] // 2
    terms = dot(attn[...], w[...], 1, 1)

    def put(source, target, top):
        if source.shape[0] == target.shape[0]:
            target[...] = (terms + source[...].astype(f32)).astype(bf16)
        else:
            place, other = slice(0, half), slice(half, 2 * half)
            if not top:
                place, other = other, place
            target[place, :] = (terms[place] + source[...].astype(f32)).astype(bf16)
            target[other, :] = terms[other].astype(bf16)

    @pl.when(pl.program_id(0) == 0)
    def _():
        put(from_left, to_right, True)

    @pl.when(pl.program_id(0) == 1)
    def _():
        put(from_right, to_left, False)


def last_body(me, attn, w, from_left, from_right, out):
    terms = dot(attn[...], w[...], 1, 1)
    out[...] = (terms + from_left[...].astype(f32) + from_right[...].astype(f32)).astype(bf16)


def ring_call(body, outs, me, attn, w, rest, offsets, name):
    ring = w.shape[0] // attn.shape[0]
    wide = w.shape[0] // ring

    def weight(i, me):
        offset = offsets[0] if len(offsets) == 1 else jnp.where(i == 0, offsets[0], offsets[1])
        return (lax.rem(me[0] + offset, ring), 0)

    specs = ([None, pl.BlockSpec((wide, w.shape[1]), weight)] + [None] * len(rest), [None] * len(outs))
    return call(body, outs, [me, attn, w] + rest, name, (len(offsets),), specs, 1)


def shift(x, axis, amount):
    count = lax.axis_size(axis)
    return lax.ppermute(x, axis, [(i, (i + amount) % count) for i in range(count)])


SIDE = 4


def torus(x, dx, dy):
    pairs = []
    for i in range(lax.axis_size("seq")):
        chip, core = i // 2, i % 2
        to = (chip // SIDE + dx) % SIDE * SIDE + (chip % SIDE + dy) % SIDE
        pairs.append((i, 2 * to + core))
    return lax.ppermute(x, "seq", pairs)


def ways(arrays, flip):
    moves = ((1, 0), (-1, 0), (0, 1), (0, -1))
    moves = moves[2:] + moves[:2] if flip else moves
    return [torus(x, *move) for x, move in zip(arrays, moves)]


tie = lax.optimization_barrier


def per_device(queries, keys, values, w_out, grad_out):
    length, features = queries.shape
    heads = features // DH
    half = length // 2
    ring = lax.axis_size("head")
    count = lax.axis_size("seq")
    at = lax.axis_index("seq")
    me = jnp.stack([lax.axis_index("head"), at % 2, at // 2 // SIDE, at // 2 % SIDE])
    me = me.astype(jnp.int32)
    block = shape((length, features), bf16)
    half_block = shape((half, features), bf16)
    wide_block = shape((length, features), f32)
    states = shape((heads, DH, DH), f32)
    tall = columns(length)

    def exchange(parts):
        return lax.all_to_all(parts, "seq", 0, 0, tiled=True)

    def sums(parts, reverse, name):
        return call(functools.partial(prefix_body, reverse), [shape(parts.shape, f32)], [parts], name)[0]

    def pieces_of(state):
        return state.reshape(count, -1, DH)

    gathered = lax.all_gather(grad_out, "head")

    (local_state,) = call(
        state_body, [states], [keys, values], "state", (heads,), ([tall, tall], [per_head()])
    )
    prefix = exchange(sums(exchange(pieces_of(local_state)), False, "prefix")).reshape(states.shape)
    attn, attn_t, mixed = call(
        forward_body,
        [block, shape((features, length), bf16), wide_block],
        [queries, keys, values, prefix],
        "forward",
        (heads,),
        (
            [tall, tall, tall, per_head()],
            [tall, pl.BlockSpec((DH, length), lambda h: (h, 0)), tall],
        ),
    )

    def hop(pair):
        return [shift(pair[0], "head", 1), shift(pair[1], "head", -1)]

    def out_step(pair, number):
        offsets = [number, ring - number]
        return ring_call(step_body, [block, block], me, attn, w_out, pair, offsets, "out_step")

    pair = ring_call(
        first_body, [half_block, half_block], me, attn, w_out, [], [ring // 2], "out_first"
    )
    pair = out_step(hop(pair), ring // 2 - 1)
    gathered, *pair = tie((gathered, *pair))
    pair_two = hop(pair)

    d_mixed, local_grads = call(
        project_body,
        [block, states],
        [gathered, w_out, mixed, queries],
        "project",
        (ring // 2,),
        (
            [
                pl.BlockSpec((2, length, features), lambda i: (i, 0, 0)),
                pl.BlockSpec((2 * features, features), lambda i: (i, 0)),
                None,
                None,
            ],
            [None, None],
        ),
        scratch=[pltpu.VMEM((length, features), f32)],
        weight=LIGHT,
    )
    wide = w_out.shape[0] // count
    dims = (count // 2, features, wide)
    chips = count // 2 // ring
    piece = pl.BlockSpec((chips, features, wide), lambda i, me: (i, 0, 0))
    gathered, d_mixed, local_grads = tie((gathered, d_mixed, local_grads))
    keep, send = call(
        weight_body,
        [shape(dims, f32), shape(dims, bf16)],
        [me, attn_t, gathered],
        "weight",
        (ring,),
        (
            [None, pl.BlockSpec((1, length, features), lambda i, me: (i, 0, 0))],
            [piece, piece],
        ),
        1,
        weight=LIGHT,
    )
    received = lax.ppermute(send, "seq", [(i, i ^ 1) for i in range(count)])
    parts = exchange(pieces_of(local_grads))

    grid_dims = (SIDE, SIDE, features, wide)

    def row(i, me):
        dx = jnp.where(i == 0, ORDER[0], jnp.where(i == 1, ORDER[1], jnp.where(i == 2, ORDER[2], 0)))
        return (lax.rem(me[2] + dx, SIDE), 0, 0, 0)

    strip = pl.BlockSpec((1,) + grid_dims[1:], row)
    far_dims = shape((SIDE // 2, features // 2, wide), bf16)
    near_dims = shape((SIDE, features // 2, wide), bf16)
    terms = call(
        pair_body,
        [far_dims] * 4 + [near_dims] * 6,
        [me, keep.reshape(grid_dims), received.reshape(grid_dims)],
        "pair_add",
        (SIDE,),
        ([strip, strip], [None] * 10),
        1,
    )
    pair = out_step(pair_two, ring // 2 - 2)
    parts, *rest = tie((parts, *pair, *terms))
    pair, terms = rest[:2], rest[2:]
    pair_three = hop(pair)
    later = exchange(sums(parts, True, "suffix")).reshape(states.shape)
    got = ways(terms[:4], False)
    near = [terms[4], terms[5], terms[7], terms[8]]
    turned = call(turn_body, [near_dims] * 4, near + got, "turn")
    pair = out_step(pair_three, ring // 2 - 3)
    later, *rest = tie((later, *pair, *turned))
    pair, turned = rest[:2], rest[2:]
    pair_four = hop(pair)
    got = ways(turned, False)
    small, large = shape((features // 4, wide), f32), shape((features // 2, wide), f32)
    terms = call(
        cross_body, [small] * 4 + [large] * 6, [terms[6], terms[9]] + got, "cross"
    )
    got = ways(terms[:4], True)
    near = [terms[4], terms[5], terms[7], terms[8]]
    got = ways(call(turn_body, [large] * 4, near + got, "turn_two"), True)
    (grad_w_out,) = call(
        close_body, [shape((wide, features), f32)], [terms[6], terms[9]] + got, "close"
    )

    grad_q, part_k, part_v = call(
        backward_body,
        [block, wide_block, wide_block],
        [queries, keys, values, d_mixed, prefix],
        "backward",
        (heads,),
        ([tall] * 4 + [per_head()], [tall] * 3),
    )
    (layer_out,) = ring_call(last_body, [block], me, attn, w_out, pair_four, [0], "out_last")
    grad_k, grad_v = call(
        finish_body,
        [block, block],
        [keys, values, part_k, part_v, later],
        "finish",
        (heads,),
        ([tall] * 4 + [per_head()], [tall] * 2),
    )
    return layer_out, grad_q, grad_k, grad_v, grad_w_out


def solution(mesh):
    return jax.shard_map(
        per_device,
        mesh=mesh,
        in_specs=(
            P("seq", "head"),
            P("seq", "head"),
            P("seq", "head"),
            P(None, "head"),
            P("seq", "head"),
        ),
        out_specs=(
            P("seq", "head"),
            P("seq", "head"),
            P("seq", "head"),
            P("seq", "head"),
            P("seq", "head"),
        ),
        check_vma=False,
    )
```

```python
import functools

import jax
import jax.numpy as jnp
from jax import lax
from jax.experimental import pallas as pl
from jax.experimental.pallas import tpu as pltpu
from jax.sharding import PartitionSpec as P

DH = 128
epsilon = 1e-06
VMEM = 63 << 20
WORK = 10**9
bf16, f32 = jnp.bfloat16, jnp.float32


def dot(a, b, left, right):
    return lax.dot_general(a, b, (((left,), (right,)), ((), ())), preferred_element_type=f32)


def split(x):
    high = x.astype(bf16)
    return high, (x - high.astype(f32)).astype(bf16)


def dot2(parts, b, left, right):
    return dot(parts[0], b, left, right) + dot(parts[1], b, left, right)


def dot2r(a, parts, left, right):
    return dot(a, parts[0], left, right) + dot(a, parts[1], left, right)


def shape(dims, dtype):
    return jax.ShapeDtypeStruct(dims, dtype)


def call(body, outs, args, name, far=(), far_outs=(), scalars=0, scratch=(), weight=1):
    specs = [pl.BlockSpec(memory_space=pltpu.SMEM)] * scalars
    for i in range(scalars, len(args)):
        specs.append(pl.BlockSpec(memory_space=pltpu.HBM if i in far else pltpu.VMEM))
    return pl.pallas_call(
        body,
        out_shape=tuple(outs),
        in_specs=specs,
        out_specs=tuple(
            pl.BlockSpec(memory_space=pltpu.HBM if i in far_outs else pltpu.VMEM)
            for i in range(len(outs))
        ),
        scratch_shapes=scratch,
        compiler_params=pltpu.CompilerParams(vmem_limit_bytes=VMEM),
        cost_estimate=pl.CostEstimate(
            flops=int(weight * WORK), bytes_accessed=1000, transcendentals=0
        ),
        name=name,
    )(*args)


def head(i):
    return slice(i * DH, (i + 1) * DH)


def state_body(left, right, out):
    for h in range(out.shape[0]):
        out[h] = dot(left[:, head(h)], right[:, head(h)], 0, 0)


def prefix_body(reverse, parts, out):
    count = parts.shape[0]
    state = jnp.zeros(parts.shape[1:], f32)
    for step in range(count):
        i = count - 1 - step if reverse else step
        out[i] = state
        state = state + parts[i]


def lower_mask(rows):
    return lax.broadcasted_iota(jnp.int32, (rows, rows), 0) >= lax.broadcasted_iota(
        jnp.int32, (rows, rows), 1
    )


def forward_body(q, k, v, prefix, attn, attn_t, mixed_out):
    rows = q.shape[0]
    mask = lower_mask(rows)
    for h in range(prefix.shape[0]):
        qh, kh, vh = q[:, head(h)], k[:, head(h)], v[:, head(h)]
        scores = split(jnp.where(mask, dot(qh, kh, 1, 1), 0.0))
        mixed = dot2(scores, vh, 1, 0) + dot2r(qh, split(prefix[h]), 1, 0)
        inverse = lax.rsqrt(jnp.mean(mixed * mixed, axis=-1, keepdims=True) + epsilon)
        normed = mixed * inverse
        mixed_out[:, head(h)] = mixed
        attn[:, head(h)] = normed.astype(bf16)
        attn_t[head(h), :] = normed.T.astype(bf16)


def project_body(me, gathered, w, mixed, q, attn_t, d_mixed, grads, keep, send, *scratch):
    blocks, weights, keeps, sends, sems, out_sems = scratch
    count, _, wide = blocks.shape
    groups = keep.shape[0] // count
    lanes = keep.shape[2]
    first = me[1] == 0
    copies, results = [], []
    for i in range(count):
        rows = pl.ds(i * wide, wide)
        copies.append(
            (
                pltpu.make_async_copy(gathered.at[i], blocks.at[i], sems.at[0, i]),
                pltpu.make_async_copy(w.at[rows, :], weights.at[rows, :], sems.at[1, i]),
            )
        )
        span = pl.ds(groups * i, groups)
        results.append(pltpu.make_async_copy(keeps.at[span], keep.at[span], out_sems.at[0, i]))
        results.append(pltpu.make_async_copy(sends.at[span], send.at[span], out_sems.at[1, i]))
    for pair in copies:
        pair[0].start()
        pair[1].start()
    total = None
    for i in range(count):
        copies[i][0].wait()
        copies[i][1].wait()
        term = dot(blocks[i], weights[i * wide : (i + 1) * wide, :], 1, 0)
        total = term if total is None else total + term
        terms = dot(attn_t[...], blocks[i], 1, 0)
        for j in range(groups):
            even = terms[:, 2 * j * lanes : (2 * j + 1) * lanes]
            odd = terms[:, (2 * j + 1) * lanes : (2 * j + 2) * lanes]
            keeps[groups * i + j] = jnp.where(first, even, odd).astype(bf16)
            sends[groups * i + j] = jnp.where(first, odd, even).astype(bf16)
        results[2 * i].start()
        results[2 * i + 1].start()
    for h in range(grads.shape[0]):
        d_attn, m = total[:, head(h)], mixed[:, head(h)]
        inverse = lax.rsqrt(jnp.mean(m * m, axis=-1, keepdims=True) + epsilon)
        normed = m * inverse
        d_m = inverse * (d_attn - normed * jnp.mean(d_attn * normed, axis=-1, keepdims=True))
        d_m = d_m.astype(bf16)
        d_mixed[:, head(h)] = d_m
        grads[h] = dot(q[:, head(h)], d_m, 0, 0)
    for copy in results:
        copy.wait()


def backward_body(q, k, v, d_mixed, prefix, grad_q, part_k, part_v):
    rows = q.shape[0]
    low = lower_mask(rows)
    high = lax.broadcasted_iota(jnp.int32, (rows, rows), 0) <= lax.broadcasted_iota(
        jnp.int32, (rows, rows), 1
    )
    for h in range(prefix.shape[0]):
        qh, kh, vh, dh = q[:, head(h)], k[:, head(h)], v[:, head(h)], d_mixed[:, head(h)]
        d_scores = split(jnp.where(low, dot(dh, vh, 1, 1), 0.0))
        grad_q[:, head(h)] = (
            dot2(d_scores, kh, 1, 0) + dot2r(dh, split(prefix[h]), 1, 1)
        ).astype(bf16)
        d_scores_t = split(jnp.where(high, dot(vh, dh, 1, 1), 0.0))
        part_k[:, head(h)] = dot2(d_scores_t, qh, 1, 0)
        scores_t = split(jnp.where(high, dot(kh, qh, 1, 1), 0.0))
        part_v[:, head(h)] = dot2(scores_t, dh, 1, 0)


def finish_body(me, k, v, part_k, part_v, states, grad_k, grad_v, held, sems):
    count = held.shape[0]
    copies = [pltpu.make_async_copy(states.at[i], held.at[i], sems.at[i]) for i in range(count)]
    for copy in copies:
        copy.start()
    for copy in copies:
        copy.wait()
    for h in range(held.shape[1]):
        later = jnp.zeros(held.shape[2:], f32)
        for i in range(count - 1, 0, -1):
            later = later + jnp.where(me[2] < i, held[i, h].astype(f32), 0.0)
        after = split(later)
        grad_k[:, head(h)] = (part_k[:, head(h)] + dot2r(v[:, head(h)], after, 1, 1)).astype(bf16)
        grad_v[:, head(h)] = (part_v[:, head(h)] + dot2r(k[:, head(h)], after, 1, 0)).astype(bf16)


def pair_body(keep, received, out):
    for i in range(keep.shape[0]):
        out[i] = (keep[i].astype(f32) + received[i].astype(f32)).astype(bf16)


def sum_body(parts, out):
    total = parts[0].astype(f32)
    for i in range(1, parts.shape[0]):
        total = total + parts[i].astype(f32)
    out[...] = total.T


def rows_of(me, w, offsets, weights, sems):
    ring = w.shape[0] // w.shape[1]
    wide = w.shape[1]
    copies = []
    for i, offset in enumerate(offsets):
        start = pl.multiple_of(lax.rem(me[0] + offset, ring) * wide, wide)
        copies.append(
            pltpu.make_async_copy(w.at[pl.ds(start, wide), :], weights.at[i], sems.at[i])
        )
    for copy in copies:
        copy.start()
    return copies


def out_body(me, attn, w, terms, top, bottom, low, high, weights, sems):
    ring = weights.shape[0]
    half = attn.shape[0] // 2
    copies = rows_of(me, w, range(ring), weights, sems)
    for i in range(ring):
        copies[i].wait()
        term = dot(attn[...], weights[i], 1, 1)
        if i == ring // 2:
            top[...] = term[:half].astype(bf16)
            bottom[...] = term[half:].astype(bf16)
        else:
            terms[i] = term
        if i == ring // 2 - 1:
            low[...] = term[half:].astype(bf16)
        if i == ring // 2 + 1:
            high[...] = term[:half].astype(bf16)


def shift(x, axis, amount):
    count = lax.axis_size(axis)
    return lax.ppermute(x, axis, [(i, (i + amount) % count) for i in range(count)])


tie = lax.optimization_barrier


def per_device(queries, keys, values, w_out, grad_out):
    length, features = queries.shape
    heads = features // DH
    half = length // 2
    ring = lax.axis_size("head")
    count = lax.axis_size("seq")
    me = jnp.stack([lax.axis_index("head"), lax.axis_index("seq") % 2, lax.axis_index("seq")])
    me = me.astype(jnp.int32)
    block = shape((length, features), bf16)
    half_block = shape((half, features), bf16)
    wide_block = shape((length, features), f32)
    states = shape((heads, DH, DH), f32)

    def exchange(parts):
        return lax.all_to_all(parts, "seq", 0, 0, tiled=True)

    def sums(parts, reverse, name):
        body = functools.partial(prefix_body, reverse)
        return call(body, [shape(parts.shape, f32)], [parts], name)[0]

    def pieces_of(state):
        return state.reshape(count, -1, DH)

    def hop(pair):
        pair = tie(tuple(pair))
        return tie((shift(pair[0], "head", 1), shift(pair[1], "head", -1)))

    def out_step(pair, number):
        outs = []
        for i, term in enumerate((terms_out[number], terms_out[ring - number])):
            got = pair[i].astype(f32)
            if got.shape[0] == half and i == 0:
                parts = [(term[:half] + got).astype(bf16), low]
                outs.append(jnp.concatenate(parts, axis=0))
            elif got.shape[0] == half:
                parts = [high, (term[half:] + got).astype(bf16)]
                outs.append(jnp.concatenate(parts, axis=0))
            else:
                outs.append((term + got).astype(bf16))
        return outs

    gathered = lax.all_gather(grad_out, "head")
    (local_state,) = call(state_body, [states], [keys, values], "state")
    prefix = exchange(sums(exchange(pieces_of(local_state)), False, "prefix")).reshape(states.shape)
    attn, attn_t, mixed = call(
        forward_body,
        [block, shape((features, length), bf16), wide_block],
        [queries, keys, values, prefix],
        "forward",
    )
    wide_terms = shape((ring, length, features), f32)
    terms_out, top, bottom, low, high = call(
        out_body,
        [wide_terms] + [half_block] * 4,
        [me, attn, w_out],
        "out_terms",
        far=(2,),
        scalars=1,
        scratch=[pltpu.VMEM((ring, features, features), bf16), pltpu.SemaphoreType.DMA((ring,))],
    )
    gathered, *pair = tie((gathered, top, bottom))
    pair = hop(pair)
    dims = (count // 2, features, w_out.shape[0] // count)
    d_mixed, local_grads, keep, send = call(
        project_body,
        [block, states, shape(dims, bf16), shape(dims, bf16)],
        [me, gathered, w_out, mixed, queries, attn_t],
        "project",
        far=(1, 2),
        far_outs=(2, 3),
        scalars=1,
        scratch=[
            pltpu.VMEM((ring, length, features), bf16),
            pltpu.VMEM(w_out.shape, bf16),
            pltpu.VMEM(dims, bf16),
            pltpu.VMEM(dims, bf16),
            pltpu.SemaphoreType.DMA((2, ring)),
            pltpu.SemaphoreType.DMA((2, ring)),
        ],
    )
    state_all = lax.all_gather(local_grads.astype(bf16), "seq")
    received = lax.ppermute(send, "seq", [(i, i ^ 1) for i in range(count)])
    (terms,) = call(pair_body, [shape(dims, bf16)], [keep, received], "pair_add")
    pair = tie((*pair, terms))[:2]
    pair = out_step(pair, ring // 2 - 1)
    after_one = tie((d_mixed, *pair))[0]
    pair = hop(pair)
    grad_q, part_k, part_v = call(
        backward_body,
        [block, wide_block, wide_block],
        [queries, keys, values, after_one, prefix],
        "backward",
    )
    terms = tie((terms, grad_q))[0]
    groups = [[2 * chip + core for chip in range(count // 2)] for core in range(2)]
    terms = lax.all_to_all(terms, "seq", 0, 0, axis_index_groups=groups, tiled=True)
    pair = tie((*pair, grad_q))[:2]
    pair = out_step(pair, ring // 2 - 2)
    pair = out_step(hop(pair), ring // 2 - 3)
    terms = tie((terms, *pair))[0]
    state_all = tie((state_all, *pair))[0]
    pair = hop(pair)
    (grad_w_out,) = call(sum_body, [shape((dims[2], dims[1]), f32)], [terms], "weight_sum")
    grad_k, grad_v = call(
        finish_body,
        [block, block],
        [me, keys, values, part_k, part_v, state_all],
        "finish",
        far=(5,),
        scalars=1,
        scratch=[pltpu.VMEM(state_all.shape, bf16), pltpu.SemaphoreType.DMA((count,))],
    )
    pair = tie((*pair, grad_k))[:2]
    layer_out = (terms_out[0] + pair[0].astype(f32) + pair[1].astype(f32)).astype(bf16)
    return layer_out, grad_q, grad_k, grad_v, grad_w_out


def solution(mesh):
    return jax.shard_map(
        per_device,
        mesh=mesh,
        in_specs=(
            P("seq", "head"),
            P("seq", "head"),
            P("seq", "head"),
            P(None, "head"),
            P("seq", "head"),
        ),
        out_specs=(
            P("seq", "head"),
            P("seq", "head"),
            P("seq", "head"),
            P("seq", "head"),
            P("seq", "head"),
        ),
        check_vma=False,
    )
```

```python
import functools

import jax
import jax.numpy as jnp
from jax import lax
from jax.experimental import pallas as pl
from jax.experimental.pallas import tpu as pltpu
from jax.sharding import PartitionSpec as P

DH = 128
epsilon = 1e-06
VMEM = 63 << 20
WORK = 10**9
bf16, f32 = jnp.bfloat16, jnp.float32


def dot(a, b, left, right):
    return lax.dot_general(a, b, (((left,), (right,)), ((), ())), preferred_element_type=f32)


def split(x):
    high = x.astype(bf16)
    return high, (x - high.astype(f32)).astype(bf16)


def dot2(parts, b, left, right):
    return dot(parts[0], b, left, right) + dot(parts[1], b, left, right)


def dot2r(a, parts, left, right):
    return dot(a, parts[0], left, right) + dot(a, parts[1], left, right)


def shape(dims, dtype):
    return jax.ShapeDtypeStruct(dims, dtype)


def call(body, outs, args, name, far=(), far_outs=(), scalars=0, scratch=(), weight=1):
    specs = [pl.BlockSpec(memory_space=pltpu.SMEM)] * scalars
    for i in range(scalars, len(args)):
        specs.append(pl.BlockSpec(memory_space=pltpu.HBM if i in far else pltpu.VMEM))
    return pl.pallas_call(
        body,
        out_shape=tuple(outs),
        in_specs=specs,
        out_specs=tuple(
            pl.BlockSpec(memory_space=pltpu.HBM if i in far_outs else pltpu.VMEM)
            for i in range(len(outs))
        ),
        scratch_shapes=scratch,
        compiler_params=pltpu.CompilerParams(vmem_limit_bytes=VMEM),
        cost_estimate=pl.CostEstimate(
            flops=int(weight * WORK), bytes_accessed=1000, transcendentals=0
        ),
        name=name,
    )(*args)


def head(i):
    return slice(i * DH, (i + 1) * DH)


def state_body(left, right, out):
    for h in range(out.shape[0]):
        out[h] = dot(left[:, head(h)], right[:, head(h)], 0, 0)


def prefix_body(reverse, parts, out):
    count = parts.shape[0]
    state = jnp.zeros(parts.shape[1:], f32)
    for step in range(count):
        i = count - 1 - step if reverse else step
        out[i] = state
        state = state + parts[i]


def lower_mask(rows):
    return lax.broadcasted_iota(jnp.int32, (rows, rows), 0) >= lax.broadcasted_iota(
        jnp.int32, (rows, rows), 1
    )


def forward_body(q, k, v, prefix, attn, attn_t, mixed_out):
    rows = q.shape[0]
    mask = lower_mask(rows)
    for h in range(prefix.shape[0]):
        qh, kh, vh = q[:, head(h)], k[:, head(h)], v[:, head(h)]
        scores = split(jnp.where(mask, dot(qh, kh, 1, 1), 0.0))
        mixed = dot2(scores, vh, 1, 0) + dot2r(qh, split(prefix[h]), 1, 0)
        inverse = lax.rsqrt(jnp.mean(mixed * mixed, axis=-1, keepdims=True) + epsilon)
        normed = mixed * inverse
        mixed_out[:, head(h)] = mixed
        attn[:, head(h)] = normed.astype(bf16)
        attn_t[head(h), :] = normed.T.astype(bf16)


def project_body(me, gathered, w, mixed, q, attn_t, d_mixed, grads, keep, send, *scratch):
    blocks, weights, keeps, sends, sems, out_sems = scratch
    count, _, wide = blocks.shape
    groups = keep.shape[0] // count
    lanes = keep.shape[2]
    first = me[1] == 0
    copies, results = [], []
    for i in range(count):
        rows = pl.ds(i * wide, wide)
        copies.append(
            (
                pltpu.make_async_copy(gathered.at[i], blocks.at[i], sems.at[0, i]),
                pltpu.make_async_copy(w.at[rows, :], weights.at[rows, :], sems.at[1, i]),
            )
        )
        span = pl.ds(groups * i, groups)
        results.append(pltpu.make_async_copy(keeps.at[span], keep.at[span], out_sems.at[0, i]))
        results.append(pltpu.make_async_copy(sends.at[span], send.at[span], out_sems.at[1, i]))
    for pair in copies:
        pair[0].start()
        pair[1].start()
    total = None
    for i in range(count):
        copies[i][0].wait()
        copies[i][1].wait()
        term = dot(blocks[i], weights[i * wide : (i + 1) * wide, :], 1, 0)
        total = term if total is None else total + term
        terms = dot(attn_t[...], blocks[i], 1, 0)
        for j in range(groups):
            even = terms[:, 2 * j * lanes : (2 * j + 1) * lanes]
            odd = terms[:, (2 * j + 1) * lanes : (2 * j + 2) * lanes]
            keeps[groups * i + j] = jnp.where(first, even, odd).astype(bf16)
            sends[groups * i + j] = jnp.where(first, odd, even).astype(bf16)
        results[2 * i].start()
        results[2 * i + 1].start()
    for h in range(grads.shape[0]):
        d_attn, m = total[:, head(h)], mixed[:, head(h)]
        inverse = lax.rsqrt(jnp.mean(m * m, axis=-1, keepdims=True) + epsilon)
        normed = m * inverse
        d_m = inverse * (d_attn - normed * jnp.mean(d_attn * normed, axis=-1, keepdims=True))
        d_m = d_m.astype(bf16)
        d_mixed[:, head(h)] = d_m
        grads[h] = dot(q[:, head(h)], d_m, 0, 0)
    for copy in results:
        copy.wait()


def backward_body(q, k, v, d_mixed, prefix, grad_q, part_k, part_v):
    rows = q.shape[0]
    low = lower_mask(rows)
    high = lax.broadcasted_iota(jnp.int32, (rows, rows), 0) <= lax.broadcasted_iota(
        jnp.int32, (rows, rows), 1
    )
    for h in range(prefix.shape[0]):
        qh, kh, vh, dh = q[:, head(h)], k[:, head(h)], v[:, head(h)], d_mixed[:, head(h)]
        d_scores = split(jnp.where(low, dot(dh, vh, 1, 1), 0.0))
        grad_q[:, head(h)] = (
            dot2(d_scores, kh, 1, 0) + dot2r(dh, split(prefix[h]), 1, 1)
        ).astype(bf16)
        d_scores_t = split(jnp.where(high, dot(vh, dh, 1, 1), 0.0))
        part_k[:, head(h)] = dot2(d_scores_t, qh, 1, 0)
        scores_t = split(jnp.where(high, dot(kh, qh, 1, 1), 0.0))
        part_v[:, head(h)] = dot2(scores_t, dh, 1, 0)


def finish_body(me, k, v, part_k, part_v, states, grad_k, grad_v, held, sems):
    count = held.shape[0]
    copies = [pltpu.make_async_copy(states.at[i], held.at[i], sems.at[i]) for i in range(count)]
    for copy in copies:
        copy.start()
    for copy in copies:
        copy.wait()
    for h in range(held.shape[1]):
        later = jnp.zeros(held.shape[2:], f32)
        for i in range(count - 1, 0, -1):
            later = later + jnp.where(me[2] < i, held[i, h].astype(f32), 0.0)
        after = split(later)
        grad_k[:, head(h)] = (part_k[:, head(h)] + dot2r(v[:, head(h)], after, 1, 1)).astype(bf16)
        grad_v[:, head(h)] = (part_v[:, head(h)] + dot2r(k[:, head(h)], after, 1, 0)).astype(bf16)


def pair_body(keep, received, out):
    for i in range(keep.shape[0]):
        out[i] = (keep[i].astype(f32) + received[i].astype(f32)).astype(bf16)


def sum_body(parts, out):
    total = parts[0].astype(f32)
    for i in range(1, parts.shape[0]):
        total = total + parts[i].astype(f32)
    out[...] = total.T


def rows_of(me, w, offsets, weights, sems):
    ring = w.shape[0] // w.shape[1]
    wide = w.shape[1]
    copies = []
    for i, offset in enumerate(offsets):
        start = pl.multiple_of(lax.rem(me[0] + offset, ring) * wide, wide)
        copies.append(
            pltpu.make_async_copy(w.at[pl.ds(start, wide), :], weights.at[i], sems.at[i])
        )
    for copy in copies:
        copy.start()
    return copies


def out_body(me, attn, w, terms, top, bottom, low, high, weights, sems):
    ring = weights.shape[0]
    half = attn.shape[0] // 2
    copies = rows_of(me, w, range(ring), weights, sems)
    for i in range(ring):
        copies[i].wait()
        term = dot(attn[...], weights[i], 1, 1)
        if i == ring // 2:
            top[...] = term[:half].astype(bf16)
            bottom[...] = term[half:].astype(bf16)
        else:
            terms[i] = term
        if i == ring // 2 - 1:
            low[...] = term[half:].astype(bf16)
        if i == ring // 2 + 1:
            high[...] = term[:half].astype(bf16)


def shift(x, axis, amount):
    count = lax.axis_size(axis)
    return lax.ppermute(x, axis, [(i, (i + amount) % count) for i in range(count)])


tie = lax.optimization_barrier


def per_device(queries, keys, values, w_out, grad_out):
    length, features = queries.shape
    heads = features // DH
    half = length // 2
    ring = lax.axis_size("head")
    count = lax.axis_size("seq")
    me = jnp.stack([lax.axis_index("head"), lax.axis_index("seq") % 2, lax.axis_index("seq")])
    me = me.astype(jnp.int32)
    block = shape((length, features), bf16)
    half_block = shape((half, features), bf16)
    wide_block = shape((length, features), f32)
    states = shape((heads, DH, DH), f32)

    def exchange(parts):
        return lax.all_to_all(parts, "seq", 0, 0, tiled=True)

    def sums(parts, reverse, name):
        body = functools.partial(prefix_body, reverse)
        return call(body, [shape(parts.shape, f32)], [parts], name)[0]

    def pieces_of(state):
        return state.reshape(count, -1, DH)

    def hop(pair):
        pair = tie(tuple(pair))
        return tie((shift(pair[0], "head", 1), shift(pair[1], "head", -1)))

    def out_step(pair, number):
        outs = []
        for i, term in enumerate((terms_out[number], terms_out[ring - number])):
            got = pair[i].astype(f32)
            if got.shape[0] == half and i == 0:
                parts = [(term[:half] + got).astype(bf16), low]
                outs.append(jnp.concatenate(parts, axis=0))
            elif got.shape[0] == half:
                parts = [high, (term[half:] + got).astype(bf16)]
                outs.append(jnp.concatenate(parts, axis=0))
            else:
                outs.append((term + got).astype(bf16))
        return outs

    gathered = lax.all_gather(grad_out, "head")
    (local_state,) = call(state_body, [states], [keys, values], "state")
    prefix = exchange(sums(exchange(pieces_of(local_state)), False, "prefix")).reshape(states.shape)
    attn, attn_t, mixed = call(
        forward_body,
        [block, shape((features, length), bf16), wide_block],
        [queries, keys, values, prefix],
        "forward",
    )
    wide_terms = shape((ring, length, features), f32)
    terms_out, top, bottom, low, high = call(
        out_body,
        [wide_terms] + [half_block] * 4,
        [me, attn, w_out],
        "out_terms",
        far=(2,),
        scalars=1,
        scratch=[pltpu.VMEM((ring, features, features), bf16), pltpu.SemaphoreType.DMA((ring,))],
    )
    gathered, *pair = tie((gathered, top, bottom))
    pair = hop(pair)
    dims = (count // 2, features, w_out.shape[0] // count)
    d_mixed, local_grads, keep, send = call(
        project_body,
        [block, states, shape(dims, bf16), shape(dims, bf16)],
        [me, gathered, w_out, mixed, queries, attn_t],
        "project",
        far=(1, 2),
        far_outs=(2, 3),
        scalars=1,
        scratch=[
            pltpu.VMEM((ring, length, features), bf16),
            pltpu.VMEM(w_out.shape, bf16),
            pltpu.VMEM(dims, bf16),
            pltpu.VMEM(dims, bf16),
            pltpu.SemaphoreType.DMA((2, ring)),
            pltpu.SemaphoreType.DMA((2, ring)),
        ],
    )
    state_all = lax.all_gather(local_grads.astype(bf16), "seq")
    received = lax.ppermute(send, "seq", [(i, i ^ 1) for i in range(count)])
    (terms,) = call(pair_body, [shape(dims, bf16)], [keep, received], "pair_add")
    pair = tie((*pair, terms))[:2]
    pair = out_step(pair, ring // 2 - 1)
    after_one = tie((d_mixed, *pair))[0]
    pair = hop(pair)
    grad_q, part_k, part_v = call(
        backward_body,
        [block, wide_block, wide_block],
        [queries, keys, values, after_one, prefix],
        "backward",
    )
    groups = [[2 * chip + core for chip in range(count // 2)] for core in range(2)]
    terms = lax.all_to_all(terms, "seq", 0, 0, axis_index_groups=groups, tiled=True)
    pair = tie((*pair, grad_q))[:2]
    pair = out_step(pair, ring // 2 - 2)
    pair = out_step(hop(pair), ring // 2 - 3)
    terms = tie((terms, *pair))[0]
    state_all = tie((state_all, *pair))[0]
    pair = hop(pair)
    (grad_w_out,) = call(sum_body, [shape((dims[2], dims[1]), f32)], [terms], "weight_sum")
    grad_k, grad_v = call(
        finish_body,
        [block, block],
        [me, keys, values, part_k, part_v, state_all],
        "finish",
        far=(5,),
        scalars=1,
        scratch=[pltpu.VMEM(state_all.shape, bf16), pltpu.SemaphoreType.DMA((count,))],
    )
    layer_out = (terms_out[0] + pair[0].astype(f32) + pair[1].astype(f32)).astype(bf16)
    return layer_out, grad_q, grad_k, grad_v, grad_w_out


def solution(mesh):
    return jax.shard_map(
        per_device,
        mesh=mesh,
        in_specs=(
            P("seq", "head"),
            P("seq", "head"),
            P("seq", "head"),
            P(None, "head"),
            P("seq", "head"),
        ),
        out_specs=(
            P("seq", "head"),
            P("seq", "head"),
            P("seq", "head"),
            P("seq", "head"),
            P("seq", "head"),
        ),
        check_vma=False,
    )
```

```python
import functools

import jax
import jax.numpy as jnp
from jax import lax
from jax.experimental import pallas as pl
from jax.experimental.pallas import tpu as pltpu
from jax.sharding import PartitionSpec as P

DH = 128
epsilon = 1e-06
VMEM = 63 << 20
WORK = 10**9
bf16, f32 = jnp.bfloat16, jnp.float32


def dot(a, b, left, right):
    return lax.dot_general(a, b, (((left,), (right,)), ((), ())), preferred_element_type=f32)


def split(x):
    high = x.astype(bf16)
    return high, (x - high.astype(f32)).astype(bf16)


def dot2(parts, b, left, right):
    return dot(parts[0], b, left, right) + dot(parts[1], b, left, right)


def dot2r(a, parts, left, right):
    return dot(a, parts[0], left, right) + dot(a, parts[1], left, right)


def shape(dims, dtype):
    return jax.ShapeDtypeStruct(dims, dtype)


def call(body, outs, args, name, far=(), far_outs=(), scalars=0, scratch=(), weight=1):
    specs = [pl.BlockSpec(memory_space=pltpu.SMEM)] * scalars
    for i in range(scalars, len(args)):
        specs.append(pl.BlockSpec(memory_space=pltpu.HBM if i in far else pltpu.VMEM))
    return pl.pallas_call(
        body,
        out_shape=tuple(outs),
        in_specs=specs,
        out_specs=tuple(
            pl.BlockSpec(memory_space=pltpu.HBM if i in far_outs else pltpu.VMEM)
            for i in range(len(outs))
        ),
        scratch_shapes=scratch,
        compiler_params=pltpu.CompilerParams(vmem_limit_bytes=VMEM),
        cost_estimate=pl.CostEstimate(
            flops=int(weight * WORK), bytes_accessed=1000, transcendentals=0
        ),
        name=name,
    )(*args)


def head(i):
    return slice(i * DH, (i + 1) * DH)


def state_body(left, right, out):
    for h in range(out.shape[0]):
        out[h] = dot(left[:, head(h)], right[:, head(h)], 0, 0)


def prefix_body(reverse, parts, out):
    count = parts.shape[0]
    state = jnp.zeros(parts.shape[1:], f32)
    for step in range(count):
        i = count - 1 - step if reverse else step
        out[i] = state
        state = state + parts[i]


def lower_mask(rows):
    return lax.broadcasted_iota(jnp.int32, (rows, rows), 0) >= lax.broadcasted_iota(
        jnp.int32, (rows, rows), 1
    )


def forward_body(q, k, v, prefix, attn, attn_t, mixed_out):
    rows = q.shape[0]
    mask = lower_mask(rows)
    for h in range(prefix.shape[0]):
        qh, kh, vh = q[:, head(h)], k[:, head(h)], v[:, head(h)]
        scores = split(jnp.where(mask, dot(qh, kh, 1, 1), 0.0))
        mixed = dot2(scores, vh, 1, 0) + dot2r(qh, split(prefix[h]), 1, 0)
        inverse = lax.rsqrt(jnp.mean(mixed * mixed, axis=-1, keepdims=True) + epsilon)
        normed = mixed * inverse
        mixed_out[:, head(h)] = mixed
        attn[:, head(h)] = normed.astype(bf16)
        attn_t[head(h), :] = normed.T.astype(bf16)


def project_body(me, gathered, w, mixed, q, attn_t, d_mixed, grads, keep, send, *scratch):
    blocks, weights, keeps, sends, sems, out_sems = scratch
    count, _, wide = blocks.shape
    groups = keep.shape[0] // count
    lanes = keep.shape[2]
    first = me[1] == 0
    copies, results = [], []
    for i in range(count):
        rows = pl.ds(i * wide, wide)
        copies.append(
            (
                pltpu.make_async_copy(gathered.at[i], blocks.at[i], sems.at[0, i]),
                pltpu.make_async_copy(w.at[rows, :], weights.at[rows, :], sems.at[1, i]),
            )
        )
        span = pl.ds(groups * i, groups)
        results.append(pltpu.make_async_copy(keeps.at[span], keep.at[span], out_sems.at[0, i]))
        results.append(pltpu.make_async_copy(sends.at[span], send.at[span], out_sems.at[1, i]))
    for pair in copies:
        pair[0].start()
        pair[1].start()
    total = None
    for i in range(count):
        copies[i][0].wait()
        copies[i][1].wait()
        term = dot(blocks[i], weights[i * wide : (i + 1) * wide, :], 1, 0)
        total = term if total is None else total + term
        terms = dot(attn_t[...], blocks[i], 1, 0)
        for j in range(groups):
            even = terms[:, 2 * j * lanes : (2 * j + 1) * lanes]
            odd = terms[:, (2 * j + 1) * lanes : (2 * j + 2) * lanes]
            keeps[groups * i + j] = jnp.where(first, even, odd).astype(bf16)
            sends[groups * i + j] = jnp.where(first, odd, even).astype(bf16)
        results[2 * i].start()
        results[2 * i + 1].start()
    for h in range(grads.shape[0]):
        d_attn, m = total[:, head(h)], mixed[:, head(h)]
        inverse = lax.rsqrt(jnp.mean(m * m, axis=-1, keepdims=True) + epsilon)
        normed = m * inverse
        d_m = inverse * (d_attn - normed * jnp.mean(d_attn * normed, axis=-1, keepdims=True))
        d_m = d_m.astype(bf16)
        d_mixed[:, head(h)] = d_m
        grads[h] = dot(q[:, head(h)], d_m, 0, 0).astype(bf16)
    for copy in results:
        copy.wait()


def backward_body(q, k, v, d_mixed, prefix, grad_q, part_k, part_v):
    rows = q.shape[0]
    low = lower_mask(rows)
    high = lax.broadcasted_iota(jnp.int32, (rows, rows), 0) <= lax.broadcasted_iota(
        jnp.int32, (rows, rows), 1
    )
    for h in range(prefix.shape[0]):
        qh, kh, vh, dh = q[:, head(h)], k[:, head(h)], v[:, head(h)], d_mixed[:, head(h)]
        d_scores = split(jnp.where(low, dot(dh, vh, 1, 1), 0.0))
        grad_q[:, head(h)] = (
            dot2(d_scores, kh, 1, 0) + dot2r(dh, split(prefix[h]), 1, 1)
        ).astype(bf16)
        d_scores_t = split(jnp.where(high, dot(vh, dh, 1, 1), 0.0))
        part_k[:, head(h)] = dot2(d_scores_t, qh, 1, 0)
        scores_t = split(jnp.where(high, dot(kh, qh, 1, 1), 0.0))
        part_v[:, head(h)] = dot2(scores_t, dh, 1, 0)


def finish_body(me, k, v, part_k, part_v, states, grad_k, grad_v, held, sems):
    count = held.shape[0]
    copies = [pltpu.make_async_copy(states.at[i], held.at[i], sems.at[i]) for i in range(count)]
    for copy in copies:
        copy.start()
    for copy in copies:
        copy.wait()
    for h in range(held.shape[1]):
        later = jnp.zeros(held.shape[2:], f32)
        for i in range(count - 1, 0, -1):
            later = later + jnp.where(me[2] < i, held[i, h].astype(f32), 0.0)
        after = split(later)
        grad_k[:, head(h)] = (part_k[:, head(h)] + dot2r(v[:, head(h)], after, 1, 1)).astype(bf16)
        grad_v[:, head(h)] = (part_v[:, head(h)] + dot2r(k[:, head(h)], after, 1, 0)).astype(bf16)


def pair_body(keep, received, out):
    for i in range(keep.shape[0]):
        out[i] = (keep[i].astype(f32) + received[i].astype(f32)).astype(bf16)


def sum_body(parts, out):
    total = parts[0].astype(f32)
    for i in range(1, parts.shape[0]):
        total = total + parts[i].astype(f32)
    out[...] = total.T


def rows_of(me, w, offsets, weights, sems):
    ring = w.shape[0] // w.shape[1]
    wide = w.shape[1]
    copies = []
    for i, offset in enumerate(offsets):
        start = pl.multiple_of(lax.rem(me[0] + offset, ring) * wide, wide)
        copies.append(
            pltpu.make_async_copy(w.at[pl.ds(start, wide), :], weights.at[i], sems.at[i])
        )
    for copy in copies:
        copy.start()
    return copies


def out_body(me, attn, w, terms, top, bottom, low, high, weights, sems):
    ring = weights.shape[0]
    half = attn.shape[0] // 2
    copies = rows_of(me, w, range(ring), weights, sems)
    for i in range(ring):
        copies[i].wait()
        term = dot(attn[...], weights[i], 1, 1)
        if i == ring // 2:
            top[...] = term[:half].astype(bf16)
            bottom[...] = term[half:].astype(bf16)
        else:
            terms[i] = term
        if i == ring // 2 - 1:
            low[...] = term[half:].astype(bf16)
        if i == ring // 2 + 1:
            high[...] = term[:half].astype(bf16)


def shift(x, axis, amount):
    count = lax.axis_size(axis)
    return lax.ppermute(x, axis, [(i, (i + amount) % count) for i in range(count)])


tie = lax.optimization_barrier


def per_device(queries, keys, values, w_out, grad_out):
    length, features = queries.shape
    heads = features // DH
    half = length // 2
    ring = lax.axis_size("head")
    count = lax.axis_size("seq")
    me = jnp.stack([lax.axis_index("head"), lax.axis_index("seq") % 2, lax.axis_index("seq")])
    me = me.astype(jnp.int32)
    block = shape((length, features), bf16)
    half_block = shape((half, features), bf16)
    wide_block = shape((length, features), f32)
    states = shape((heads, DH, DH), f32)

    def exchange(parts):
        return lax.all_to_all(parts, "seq", 0, 0, tiled=True)

    def sums(parts, reverse, name):
        body = functools.partial(prefix_body, reverse)
        return call(body, [shape(parts.shape, f32)], [parts], name)[0]

    def pieces_of(state):
        return state.reshape(count, -1, DH)

    def hop(pair):
        pair = tie(tuple(pair))
        return tie((shift(pair[0], "head", 1), shift(pair[1], "head", -1)))

    def out_step(pair, number):
        outs = []
        for i, term in enumerate((terms_out[number], terms_out[ring - number])):
            got = pair[i].astype(f32)
            if got.shape[0] == half and i == 0:
                parts = [(term[:half] + got).astype(bf16), low]
                outs.append(jnp.concatenate(parts, axis=0))
            elif got.shape[0] == half:
                parts = [high, (term[half:] + got).astype(bf16)]
                outs.append(jnp.concatenate(parts, axis=0))
            else:
                outs.append((term + got).astype(bf16))
        return outs

    gathered = lax.all_gather(grad_out, "head")
    (local_state,) = call(state_body, [states], [keys, values], "state")
    prefix = exchange(sums(exchange(pieces_of(local_state)), False, "prefix")).reshape(states.shape)
    attn, attn_t, mixed = call(
        forward_body,
        [block, shape((features, length), bf16), wide_block],
        [queries, keys, values, prefix],
        "forward",
    )
    wide_terms = shape((ring, length, features), f32)
    terms_out, top, bottom, low, high = call(
        out_body,
        [wide_terms] + [half_block] * 4,
        [me, attn, w_out],
        "out_terms",
        far=(2,),
        scalars=1,
        scratch=[pltpu.VMEM((ring, features, features), bf16), pltpu.SemaphoreType.DMA((ring,))],
    )
    gathered, *pair = tie((gathered, top, bottom))
    pair = hop(pair)
    dims = (count // 2, features, w_out.shape[0] // count)
    d_mixed, local_grads, keep, send = call(
        project_body,
        [block, shape(states.shape, bf16), shape(dims, bf16), shape(dims, bf16)],
        [me, gathered, w_out, mixed, queries, attn_t],
        "project",
        far=(1, 2),
        far_outs=(2, 3),
        scalars=1,
        scratch=[
            pltpu.VMEM((ring, length, features), bf16),
            pltpu.VMEM(w_out.shape, bf16),
            pltpu.VMEM(dims, bf16),
            pltpu.VMEM(dims, bf16),
            pltpu.SemaphoreType.DMA((2, ring)),
            pltpu.SemaphoreType.DMA((2, ring)),
        ],
    )
    state_all = lax.all_gather(local_grads, "seq")
    received = lax.ppermute(send, "seq", [(i, i ^ 1) for i in range(count)])
    (terms,) = call(pair_body, [shape(dims, bf16)], [keep, received], "pair_add")
    pair = tie((*pair, terms))[:2]
    pair = out_step(pair, ring // 2 - 1)
    pair = hop(pair)
    groups = [[2 * chip + core for chip in range(count // 2)] for core in range(2)]
    terms = lax.all_to_all(terms, "seq", 0, 0, axis_index_groups=groups, tiled=True)
    pair = out_step(pair, ring // 2 - 2)
    after_two = tie((d_mixed, *pair))[0]
    pair = hop(pair)
    grad_q, part_k, part_v = call(
        backward_body,
        [block, wide_block, wide_block],
        [queries, keys, values, after_two, prefix],
        "backward",
    )
    pair = tie((*pair, grad_q))[:2]
    pair = out_step(pair, ring // 2 - 3)
    terms = tie((terms, *pair))[0]
    state_all = tie((state_all, *pair))[0]
    pair = hop(pair)
    (grad_w_out,) = call(sum_body, [shape((dims[2], dims[1]), f32)], [terms], "weight_sum")
    grad_k, grad_v = call(
        finish_body,
        [block, block],
        [me, keys, values, part_k, part_v, state_all],
        "finish",
        far=(5,),
        scalars=1,
        scratch=[pltpu.VMEM(state_all.shape, bf16), pltpu.SemaphoreType.DMA((count,))],
    )
    layer_out = (terms_out[0] + pair[0].astype(f32) + pair[1].astype(f32)).astype(bf16)
    return layer_out, grad_q, grad_k, grad_v, grad_w_out


def solution(mesh):
    return jax.shard_map(
        per_device,
        mesh=mesh,
        in_specs=(
            P("seq", "head"),
            P("seq", "head"),
            P("seq", "head"),
            P(None, "head"),
            P("seq", "head"),
        ),
        out_specs=(
            P("seq", "head"),
            P("seq", "head"),
            P("seq", "head"),
            P("seq", "head"),
            P("seq", "head"),
        ),
        check_vma=False,
    )
```

```python
import functools

import jax
import jax.numpy as jnp
from jax import lax
from jax.experimental import pallas as pl
from jax.experimental.pallas import tpu as pltpu
from jax.sharding import PartitionSpec as P

DH = 128
epsilon = 1e-06
VMEM = 63 << 20
WORK = 10**9
bf16, f32 = jnp.bfloat16, jnp.float32


def dot(a, b, left, right):
    return lax.dot_general(a, b, (((left,), (right,)), ((), ())), preferred_element_type=f32)


def split(x):
    high = x.astype(bf16)
    return high, (x - high.astype(f32)).astype(bf16)


def dot2(parts, b, left, right):
    return dot(parts[0], b, left, right) + dot(parts[1], b, left, right)


def dot2r(a, parts, left, right):
    return dot(a, parts[0], left, right) + dot(a, parts[1], left, right)


def shape(dims, dtype):
    return jax.ShapeDtypeStruct(dims, dtype)


def call(body, outs, args, name, far=(), far_outs=(), scalars=0, scratch=(), weight=1):
    specs = [pl.BlockSpec(memory_space=pltpu.SMEM)] * scalars
    for i in range(scalars, len(args)):
        specs.append(pl.BlockSpec(memory_space=pltpu.HBM if i in far else pltpu.VMEM))
    return pl.pallas_call(
        body,
        out_shape=tuple(outs),
        in_specs=specs,
        out_specs=tuple(
            pl.BlockSpec(memory_space=pltpu.HBM if i in far_outs else pltpu.VMEM)
            for i in range(len(outs))
        ),
        scratch_shapes=scratch,
        compiler_params=pltpu.CompilerParams(vmem_limit_bytes=VMEM),
        cost_estimate=pl.CostEstimate(
            flops=int(weight * WORK), bytes_accessed=1000, transcendentals=0
        ),
        name=name,
    )(*args)


def head(i):
    return slice(i * DH, (i + 1) * DH)


def state_body(left, right, out):
    for h in range(out.shape[0]):
        out[h] = dot(left[:, head(h)], right[:, head(h)], 0, 0)


def prefix_body(reverse, parts, out):
    count = parts.shape[0]
    state = jnp.zeros(parts.shape[1:], f32)
    for step in range(count):
        i = count - 1 - step if reverse else step
        out[i] = state
        state = state + parts[i]


def lower_mask(rows):
    return lax.broadcasted_iota(jnp.int32, (rows, rows), 0) >= lax.broadcasted_iota(
        jnp.int32, (rows, rows), 1
    )


def forward_body(q, k, v, prefix, attn, attn_t, mixed_out):
    rows = q.shape[0]
    mask = lower_mask(rows)
    for h in range(prefix.shape[0]):
        qh, kh, vh = q[:, head(h)], k[:, head(h)], v[:, head(h)]
        scores = split(jnp.where(mask, dot(qh, kh, 1, 1), 0.0))
        mixed = dot2(scores, vh, 1, 0) + dot2r(qh, split(prefix[h]), 1, 0)
        inverse = lax.rsqrt(jnp.mean(mixed * mixed, axis=-1, keepdims=True) + epsilon)
        normed = mixed * inverse
        mixed_out[:, head(h)] = mixed
        attn[:, head(h)] = normed.astype(bf16)
        attn_t[head(h), :] = normed.T.astype(bf16)


def project_body(me, gathered, w, mixed, q, attn_t, d_mixed, grads, keep, send, *scratch):
    blocks, weights, keeps, sends, sems, out_sems = scratch
    count, _, wide = blocks.shape
    groups = keep.shape[0] // count
    lanes = keep.shape[2]
    first = me[1] == 0
    copies, results = [], []
    for i in range(count):
        rows = pl.ds(i * wide, wide)
        copies.append(
            (
                pltpu.make_async_copy(gathered.at[i], blocks.at[i], sems.at[0, i]),
                pltpu.make_async_copy(w.at[rows, :], weights.at[rows, :], sems.at[1, i]),
            )
        )
        span = pl.ds(groups * i, groups)
        results.append(pltpu.make_async_copy(keeps.at[span], keep.at[span], out_sems.at[0, i]))
        results.append(pltpu.make_async_copy(sends.at[span], send.at[span], out_sems.at[1, i]))
    for pair in copies:
        pair[0].start()
        pair[1].start()
    total = None
    for i in range(count):
        copies[i][0].wait()
        copies[i][1].wait()
        term = dot(blocks[i], weights[i * wide : (i + 1) * wide, :], 1, 0)
        total = term if total is None else total + term
        terms = dot(attn_t[...], blocks[i], 1, 0)
        for j in range(groups):
            even = terms[:, 2 * j * lanes : (2 * j + 1) * lanes]
            odd = terms[:, (2 * j + 1) * lanes : (2 * j + 2) * lanes]
            keeps[groups * i + j] = jnp.where(first, even, odd).astype(bf16)
            sends[groups * i + j] = jnp.where(first, odd, even).astype(bf16)
        results[2 * i].start()
        results[2 * i + 1].start()
    for h in range(grads.shape[0]):
        d_attn, m = total[:, head(h)], mixed[:, head(h)]
        inverse = lax.rsqrt(jnp.mean(m * m, axis=-1, keepdims=True) + epsilon)
        normed = m * inverse
        d_m = inverse * (d_attn - normed * jnp.mean(d_attn * normed, axis=-1, keepdims=True))
        d_m = d_m.astype(bf16)
        d_mixed[:, head(h)] = d_m
        grads[h] = dot(q[:, head(h)], d_m, 0, 0).astype(bf16)
    for copy in results:
        copy.wait()


def backward_body(q, k, v, d_mixed, prefix, grad_q, part_k, part_v):
    rows = q.shape[0]
    low = lower_mask(rows)
    high = lax.broadcasted_iota(jnp.int32, (rows, rows), 0) <= lax.broadcasted_iota(
        jnp.int32, (rows, rows), 1
    )
    for h in range(prefix.shape[0]):
        qh, kh, vh, dh = q[:, head(h)], k[:, head(h)], v[:, head(h)], d_mixed[:, head(h)]
        d_scores = split(jnp.where(low, dot(dh, vh, 1, 1), 0.0))
        grad_q[:, head(h)] = (
            dot2(d_scores, kh, 1, 0) + dot2r(dh, split(prefix[h]), 1, 1)
        ).astype(bf16)
        d_scores_t = split(jnp.where(high, dot(vh, dh, 1, 1), 0.0))
        part_k[:, head(h)] = dot2(d_scores_t, qh, 1, 0)
        scores_t = split(jnp.where(high, dot(kh, qh, 1, 1), 0.0))
        part_v[:, head(h)] = dot2(scores_t, dh, 1, 0)


def finish_body(me, k, v, part_k, part_v, states, grad_k, grad_v, held, sems):
    count = held.shape[0]
    copies = [pltpu.make_async_copy(states.at[i], held.at[i], sems.at[i]) for i in range(count)]
    for copy in copies:
        copy.start()
    for copy in copies:
        copy.wait()
    for h in range(held.shape[1]):
        later = jnp.zeros(held.shape[2:], f32)
        for i in range(count - 1, 0, -1):
            later = later + jnp.where(me[2] < i, held[i, h].astype(f32), 0.0)
        after = split(later)
        grad_k[:, head(h)] = (part_k[:, head(h)] + dot2r(v[:, head(h)], after, 1, 1)).astype(bf16)
        grad_v[:, head(h)] = (part_v[:, head(h)] + dot2r(k[:, head(h)], after, 1, 0)).astype(bf16)


def pair_body(keep, received, out):
    for i in range(keep.shape[0]):
        out[i] = (keep[i].astype(f32) + received[i].astype(f32)).astype(bf16)


def sum_body(parts, out):
    total = parts[0].astype(f32)
    for i in range(1, parts.shape[0]):
        total = total + parts[i].astype(f32)
    out[...] = total.T


def rows_of(me, w, offsets, weights, sems):
    ring = w.shape[0] // w.shape[1]
    wide = w.shape[1]
    copies = []
    for i, offset in enumerate(offsets):
        start = pl.multiple_of(lax.rem(me[0] + offset, ring) * wide, wide)
        copies.append(
            pltpu.make_async_copy(w.at[pl.ds(start, wide), :], weights.at[i], sems.at[i])
        )
    for copy in copies:
        copy.start()
    return copies


def out_body(me, attn, w, terms, top, bottom, low, high, weights, sems):
    ring = weights.shape[0]
    half = attn.shape[0] // 2
    copies = rows_of(me, w, range(ring), weights, sems)
    for i in range(ring):
        copies[i].wait()
        term = dot(attn[...], weights[i], 1, 1)
        if i == ring // 2:
            top[...] = term[:half].astype(bf16)
            bottom[...] = term[half:].astype(bf16)
        else:
            terms[i] = term
        if i == ring // 2 - 1:
            low[...] = term[half:].astype(bf16)
        if i == ring // 2 + 1:
            high[...] = term[:half].astype(bf16)


def shift(x, axis, amount):
    count = lax.axis_size(axis)
    return lax.ppermute(x, axis, [(i, (i + amount) % count) for i in range(count)])


tie = lax.optimization_barrier


def per_device(queries, keys, values, w_out, grad_out):
    length, features = queries.shape
    heads = features // DH
    half = length // 2
    ring = lax.axis_size("head")
    count = lax.axis_size("seq")
    me = jnp.stack([lax.axis_index("head"), lax.axis_index("seq") % 2, lax.axis_index("seq")])
    me = me.astype(jnp.int32)
    block = shape((length, features), bf16)
    half_block = shape((half, features), bf16)
    wide_block = shape((length, features), f32)
    states = shape((heads, DH, DH), f32)

    def exchange(parts):
        return lax.all_to_all(parts, "seq", 0, 0, tiled=True)

    def sums(parts, reverse, name):
        body = functools.partial(prefix_body, reverse)
        return call(body, [shape(parts.shape, f32)], [parts], name)[0]

    def pieces_of(state):
        return state.reshape(count, -1, DH)

    def hop(pair):
        pair = tie(tuple(pair))
        return tie((shift(pair[0], "head", 1), shift(pair[1], "head", -1)))

    def out_step(pair, number):
        outs = []
        for i, term in enumerate((terms_out[number], terms_out[ring - number])):
            got = pair[i].astype(f32)
            if got.shape[0] == half and i == 0:
                parts = [(term[:half] + got).astype(bf16), low]
                outs.append(jnp.concatenate(parts, axis=0))
            elif got.shape[0] == half:
                parts = [high, (term[half:] + got).astype(bf16)]
                outs.append(jnp.concatenate(parts, axis=0))
            else:
                outs.append((term + got).astype(bf16))
        return outs

    gathered = lax.all_gather(grad_out, "head")
    (local_state,) = call(state_body, [states], [keys, values], "state")
    prefix = exchange(sums(exchange(pieces_of(local_state)), False, "prefix")).reshape(states.shape)
    attn, attn_t, mixed = call(
        forward_body,
        [block, shape((features, length), bf16), wide_block],
        [queries, keys, values, prefix],
        "forward",
    )
    wide_terms = shape((ring, length, features), f32)
    terms_out, top, bottom, low, high = call(
        out_body,
        [wide_terms] + [half_block] * 4,
        [me, attn, w_out],
        "out_terms",
        far=(2,),
        scalars=1,
        scratch=[pltpu.VMEM((ring, features, features), bf16), pltpu.SemaphoreType.DMA((ring,))],
    )
    gathered, *pair = tie((gathered, top, bottom))
    pair = hop(pair)
    dims = (count // 2, features, w_out.shape[0] // count)
    d_mixed, local_grads, keep, send = call(
        project_body,
        [block, shape(states.shape, bf16), shape(dims, bf16), shape(dims, bf16)],
        [me, gathered, w_out, mixed, queries, attn_t],
        "project",
        far=(1, 2),
        far_outs=(2, 3),
        scalars=1,
        scratch=[
            pltpu.VMEM((ring, length, features), bf16),
            pltpu.VMEM(w_out.shape, bf16),
            pltpu.VMEM(dims, bf16),
            pltpu.VMEM(dims, bf16),
            pltpu.SemaphoreType.DMA((2, ring)),
            pltpu.SemaphoreType.DMA((2, ring)),
        ],
    )
    state_all = lax.all_gather(local_grads, "seq")
    received = lax.ppermute(send, "seq", [(i, i ^ 1) for i in range(count)])
    pair = out_step(pair, ring // 2 - 1)
    keep = tie((keep, *pair))[0]
    (terms,) = call(pair_body, [shape(dims, bf16)], [keep, received], "pair_add")
    pair = hop(pair)
    groups = [[2 * chip + core for chip in range(count // 2)] for core in range(2)]
    terms = lax.all_to_all(terms, "seq", 0, 0, axis_index_groups=groups, tiled=True)
    pair = out_step(pair, ring // 2 - 2)
    after_two = tie((d_mixed, *pair))[0]
    pair = hop(pair)
    grad_q, part_k, part_v = call(
        backward_body,
        [block, wide_block, wide_block],
        [queries, keys, values, after_two, prefix],
        "backward",
    )
    pair = tie((*pair, grad_q))[:2]
    pair = out_step(pair, ring // 2 - 3)
    terms = tie((terms, *pair))[0]
    state_all = tie((state_all, *pair))[0]
    pair = hop(pair)
    (grad_w_out,) = call(sum_body, [shape((dims[2], dims[1]), f32)], [terms], "weight_sum")
    grad_k, grad_v = call(
        finish_body,
        [block, block],
        [me, keys, values, part_k, part_v, state_all],
        "finish",
        far=(5,),
        scalars=1,
        scratch=[pltpu.VMEM(state_all.shape, bf16), pltpu.SemaphoreType.DMA((count,))],
    )
    layer_out = (terms_out[0] + pair[0].astype(f32) + pair[1].astype(f32)).astype(bf16)
    return layer_out, grad_q, grad_k, grad_v, grad_w_out


def solution(mesh):
    return jax.shard_map(
        per_device,
        mesh=mesh,
        in_specs=(
            P("seq", "head"),
            P("seq", "head"),
            P("seq", "head"),
            P(None, "head"),
            P("seq", "head"),
        ),
        out_specs=(
            P("seq", "head"),
            P("seq", "head"),
            P("seq", "head"),
            P("seq", "head"),
            P("seq", "head"),
        ),
        check_vma=False,
    )
```
